512 devices in a mesh: dp: 32 (over z, core), head: 16 (over x, y).
Axes of the slice: x: 4, y: 4, z: 16, core: 2. Of those that a mesh axis runs over, the one named last changes fastest.
Arguments:
- queries: bfloat16 [24576, 4096], P(('dp', 'head')), may hold values from -35 to 35
- keys: bfloat16 [24576, 4096], P(('dp', 'head')), may hold values from -10 to 10
- values: bfloat16 [24576, 4096], P(('dp', 'head')), may hold values from -6 to 6
- key_tiles: int32 [64, 6], P('dp'), may hold values from 0 to 63, as said below
- key_counts: int32 [64], P('dp'), may hold values from 1 to 6, as said below
- out_weight: bfloat16 [4096, 6144], P('dp', 'head'), may hold values from -0.09375 to 0.09375
Outputs:
- projected: bfloat16 [24576, 6144], P('dp', 'head')
The draws below stay inside these ranges and needn't reach their ends.
Inputs may be any that keep to these rules, and one draw needn't show every extreme that they name: `key_tiles`: row t lists tiles whose tile row and tile-frame each differ from those of t by at most 1; entry 0 is t itself; the first key_counts[t] entries are distinct, and the later ones repeat t. `key_counts`: at most the number of tiles whose tile row and tile-frame each differ from those of the tile by at most 1; some tile has 6 in every draw.
All inputs are finite; a program needn't handle non-finite values.
Results may differ from the reference program's by a relative error of at most 0.0056.
Values may be sent and summed in bfloat16 or wider, within the bound.
A program may use at most 64 MiB of HBM per device.

```python
import jax
import jax.numpy as jnp
from jax import lax

D = 6144
HEADS = 32
HD = 128
TILE = 384
GRID_F = 2
KMAX = 6
TILES_GRP = 2
TILES = 64
TOKENS = 24576
N_DP = 32


def tile_lists(key):
    key = jax.random.fold_in(key, 11)
    offsets = jnp.arange(9, dtype=jnp.int32)
    row_step = offsets // 3 - 1
    frame_step = offsets % 3 - 1
    tile_rows = TILES // GRID_F
    query_index = jnp.arange(TILES, dtype=jnp.int32)[:, None]
    cand_row = query_index // GRID_F + row_step[None, :]
    cand_frame = query_index % GRID_F + frame_step[None, :]
    in_range = (cand_row >= 0) & (cand_row < tile_rows) & (cand_frame >= 0) & (cand_frame < GRID_F)
    candidates = jnp.where(in_range, cand_row * GRID_F + cand_frame, query_index)
    ranking = jax.random.randint(jax.random.fold_in(key, 1), (TILES, 9), 0, 1 << 20, dtype=jnp.int32) * 9
    ranking = ranking + offsets[None, :]
    ranking = jnp.where((row_step[None, :] == 0) & (frame_step[None, :] == 0), -1, ranking)
    ranking = jnp.where(in_range, ranking, 1 << 30)
    sorted_order = jnp.argsort(ranking, axis=1, stable=True)
    listed = jnp.take_along_axis(candidates, sorted_order, axis=1)[:, :KMAX]
    available = jnp.minimum(jnp.sum(in_range.astype(jnp.int32), axis=1), KMAX)
    group_level = jax.random.randint(jax.random.fold_in(key, 2), (N_DP,), 1, KMAX + 1, dtype=jnp.int32)
    wanted = jnp.repeat(group_level, TILES_GRP) + jax.random.randint(jax.random.fold_in(key, 3), (TILES,), -1, 2, dtype=jnp.int32)
    live_count = jnp.clip(wanted, 1, available)
    full_tile = jax.random.randint(jax.random.fold_in(key, 4), (), GRID_F, TILES - GRID_F, dtype=jnp.int32)
    live_count = jnp.where(query_index[:, 0] == full_tile, KMAX, live_count)
    slots = jnp.arange(KMAX, dtype=jnp.int32)[None, :]
    listed = jnp.where(slots < live_count[:, None], listed, query_index)
    return (listed.astype(jnp.int32), live_count.astype(jnp.int32))


def draw_key_tiles(key, part):
    return tile_lists(key)[0]


def draw_key_counts(key, part):
    return tile_lists(key)[1]


def draw_queries(key, part):
    key = jax.random.fold_in(key, 3)
    return jax.random.normal(key, (TOKENS, HEADS * HD), jnp.float32).astype(jnp.bfloat16)


def draw_keys(key, part):
    key = jax.random.fold_in(key, 4)
    return jax.random.normal(key, (TOKENS, HEADS * HD), jnp.float32).astype(jnp.bfloat16)


def steps_of(own_key, extent, split, least, largest):
    factor_of, own = 1.0, jax.random.fold_in(own_key, 6)
    for axis_at, parts in split:
        draws = jnp.exp(jax.random.uniform(jax.random.fold_in(own, axis_at), (parts,), jnp.float32, least / len(split), largest / len(split)))
        factor_of = factor_of * jnp.repeat(draws, extent[axis_at] // parts).reshape([-1 if axis == axis_at else 1 for axis in range(len(extent))])
    return factor_of


def noise(own_key, extent, width, reach, pieces=(), held_as=jnp.bfloat16):
    array = jax.random.normal(own_key, extent, jnp.float32) * width
    if len(pieces) > 0:
        array = steps_of(own_key, extent, pieces, -0.22, 0.18) * array
    return jnp.clip(array, min=-reach, max=reach).astype(held_as)


def setup_inputs(seed: int = 0) -> dict:
    seeds = jax.random.split(jax.random.key(seed), 7)
    return {
        "queries": draw_queries(jax.random.fold_in(seeds[6], 71), 0),
        "keys": draw_keys(jax.random.fold_in(seeds[6], 71), 0),
        "values": noise(seeds[2], (TOKENS, HEADS * HD), 1.0, 6.0, ((0, 512),)),
        "key_tiles": draw_key_tiles(jax.random.fold_in(seeds[6], 71), 0),
        "key_counts": draw_key_counts(jax.random.fold_in(seeds[6], 71), 0),
        "out_weight": noise(seeds[5], (HEADS * HD, D), (HEADS * HD) ** -0.5, 0.09375, ((0, 32), (1, 16))),
    }


def reference(queries, keys, values, key_tiles, key_counts, out_weight):
    query_grid = queries.reshape(TILES, TILE, HEADS, HD)
    key_grid = keys.reshape(TILES, TILE, HEADS, HD)
    value_grid = values.reshape(TILES, TILE, HEADS, HD)
    score_scale = HD ** -0.5

    def attend(inputs):
        tile_index, listed, live_count = inputs
        query_tile = query_grid[tile_index].astype(jnp.float32)
        key_all = key_grid[listed].reshape(KMAX * TILE, HEADS, HD).astype(jnp.float32)
        value_all = value_grid[listed].reshape(KMAX * TILE, HEADS, HD).astype(jnp.float32)
        scored = jnp.einsum("qhd,khd->hqk", query_tile, key_all, precision=lax.Precision.HIGHEST) * score_scale
        live_mask = jnp.repeat(jnp.arange(KMAX) < live_count, TILE)
        scored = jnp.where(live_mask[None, None, :], scored, -jnp.inf)
        peak_score = jnp.max(scored, axis=2, keepdims=True)
        weights = jnp.exp(scored - peak_score)
        denominator = jnp.sum(weights, axis=2)
        rounded = lax.optimization_barrier(weights.astype(jnp.bfloat16)).astype(jnp.float32)
        weighted = jnp.einsum("hqk,khd->hqd", rounded, value_all, precision=lax.Precision.HIGHEST)
        attended = (weighted / denominator[:, :, None]).astype(jnp.bfloat16)
        return jnp.transpose(attended, (1, 0, 2))

    attended = lax.map(attend, (jnp.arange(TILES).astype(jnp.int32), key_tiles, key_counts))
    flat = attended.reshape(TOKENS, HEADS * HD)
    return jnp.dot(flat, out_weight, preferred_element_type=jnp.float32).astype(jnp.bfloat16)
```

```python
import math

import jax
import jax.numpy as jnp
from jax import lax
from jax.experimental import pallas as pl
from jax.experimental.pallas import tpu as pltpu
from jax.sharding import PartitionSpec as P

HD = 128
TILE = 384
KMAX = 6
GRID_F = 2
ROWS = 768
TOK = 48
PAIR = 256
COLS = 384
DEAD = 1e30
MESH = pl.DeviceIdType.MESH


def kernel(
    tiles_ref, counts_ref, q_hbm, k_hbm, v_hbm, w_hbm, out_ref,
    q_rows, k_ext, v_ext, wbuf, agat, pc, rc, acc,
    local_sem, a2a_send, a2a_recv, halo_send, halo_recv,
    xr_send, xr_recv, plus_send, plus_recv, minus_send, minus_recv, sib_send, sib_recv,
    gat_send, gat_recv, rs_send, rs_recv,
):
    dp = lax.axis_index("dp")
    h = lax.axis_index("head")
    z, c = dp // 2, dp % 2
    x, y = h // 4, h % 4
    sibling = dp + 1 - 2 * c

    def remote(src, dst, send, recv, dp_to, h_to):
        return pltpu.make_async_remote_copy(
            src_ref=src, dst_ref=dst, send_sem=send, recv_sem=recv, device_id=(dp_to, h_to), device_id_type=MESH
        )

    barrier = pltpu.get_barrier_semaphore()

    def greet(i, carry):
        pl.semaphore_signal(barrier, inc=1, device_id=(dp, (h + i) % 16), device_id_type=MESH)
        return carry

    lax.fori_loop(1, 16, greet, 0)
    for step in (1, 2, 30, 31):
        pl.semaphore_signal(barrier, inc=1, device_id=((dp + step) % 32, h), device_id_type=MESH)
    pl.semaphore_wait(barrier, 19)

    own_rows = pl.ds(pl.multiple_of(128 * (2 * (z // 4) + c), 128), 128)
    ring_x = z % 4
    is_src = ring_x == x

    def xr_copy():
        return remote(w_hbm, wbuf.at[x, own_rows], xr_send, xr_recv.at[x], dp, 4 * ring_x + y)

    w_local = pltpu.make_async_copy(w_hbm, wbuf.at[x, own_rows], local_sem.at[3])

    @pl.when(is_src)
    def _():
        w_local.start()

    @pl.when(jnp.logical_not(is_src))
    def _():
        xr_copy().start()

    sources = (k_hbm, v_hbm, q_hbm)
    targets = (k_ext, v_ext, q_rows)
    bases = (ROWS, ROWS, 0)

    def columns_of(head_to):
        return pl.ds(pl.multiple_of(PAIR * (head_to // 4 + 4 * (head_to % 4)), PAIR), PAIR)

    def land(a, head_from):
        return targets[a].at[pl.ds(pl.multiple_of(bases[a] + TOK * head_from, 16), TOK)]

    def a2a_copy(a, i):
        to = (h + i) % 16
        return remote(sources[a].at[:, columns_of(to)], land(a, h), a2a_send.at[a, i], a2a_recv.at[a, i], dp, to)

    def own_copy(a):
        return pltpu.make_async_copy(sources[a].at[:, columns_of(h)], land(a, h), local_sem.at[a])

    for a in range(3):
        own_copy(a).start()

        def start_one(i, carry, a=a):
            a2a_copy(a, i).start()
            return carry

        lax.fori_loop(1, 16, start_one, 0)

    def a2a_wait(a):
        own_copy(a).wait()

        def wait_one(i, carry):
            a2a_copy(a, i).wait_recv()
            return carry

        lax.fori_loop(1, 16, wait_one, 0)

    middle = pl.ds(ROWS, ROWS)
    sides = (pl.ds(0, ROWS), pl.ds(2 * ROWS, ROWS))

    def halo_copy(a, side):
        return remote(
            targets[a].at[middle], targets[a].at[sides[side]], halo_send.at[a, side], halo_recv.at[a, side],
            (dp + 1 + 30 * side) % 32, h,
        )

    has_next, has_prev = dp < 31, dp > 0

    def halo_start(a):
        @pl.when(has_next)
        def _():
            halo_copy(a, 0).start()

        @pl.when(has_prev)
        def _():
            halo_copy(a, 1).start()

    def halo_wait_recv(a):
        @pl.when(has_prev)
        def _():
            halo_copy(a, 0).wait_recv()

        @pl.when(has_next)
        def _():
            halo_copy(a, 1).wait_recv()

    def halo_wait_send(a):
        @pl.when(has_next)
        def _():
            halo_copy(a, 0).wait_send()

        @pl.when(has_prev)
        def _():
            halo_copy(a, 1).wait_send()

    @pl.when(jnp.logical_not(has_prev))
    def _():
        k_ext[0:ROWS, :] = jnp.zeros((ROWS, PAIR), jnp.bfloat16)
        v_ext[0:ROWS, :] = jnp.zeros((ROWS, PAIR), jnp.bfloat16)

    @pl.when(jnp.logical_not(has_next))
    def _():
        k_ext[2 * ROWS : 3 * ROWS, :] = jnp.zeros((ROWS, PAIR), jnp.bfloat16)
        v_ext[2 * ROWS : 3 * ROWS, :] = jnp.zeros((ROWS, PAIR), jnp.bfloat16)

    ahead = (z - x + 16) % 4
    behind = (x - z + 16) % 4
    ahead_from = (ahead + 3) % 4 + 1
    behind_from = (behind + 3) % 4 + 1
    dp_plus, dp_minus = (dp + 2) % 32, (dp + 30) % 32

    def block(j, zs):
        return wbuf.at[j, pl.ds(pl.multiple_of(128 * (2 * (zs // 4) + c), 128), 128)]

    def plus_copy(i):
        b = block(i % 4, (z - ahead - 4 * (i // 4) + 32) % 16)
        return remote(b, b, plus_send.at[i], plus_recv.at[i], dp_plus, h)

    def plus_arrival(i):
        b = block(i % 4, (z - ahead_from - 4 * (i // 4) + 32) % 16)
        return remote(b, b, plus_send.at[i], plus_recv.at[i], dp_plus, h)

    def minus_copy(i):
        b = block(i % 4, (z + behind + 4 * (i // 4)) % 16)
        return remote(b, b, minus_send.at[i], minus_recv.at[i], dp_minus, h)

    def minus_arrival(i):
        b = block(i % 4, (z + behind_from + 4 * (i // 4)) % 16)
        return remote(b, b, minus_send.at[i], minus_recv.at[i], dp_minus, h)

    def share(j, zs, n):
        b = block(j, zs)
        return remote(b, b, sib_send.at[n], sib_recv.at[n], sibling, h)

    def share_block(j, zs):
        return share(j, zs, 4 * (zs // 4) + j)

    def pump(i):
        @pl.when(is_src)
        def _():
            if i < 4:
                @pl.when(x == i)
                def _():
                    w_local.wait()

                @pl.when(x != i)
                def _():
                    b = block(i, z)
                    remote(b, b, xr_send, xr_recv.at[i], dp, h).wait_recv()

                share_block(i, z).start()
                plus_copy(i).start()
                minus_copy(i).start()
            else:
                plus_arrival(i - 4).wait_recv()
                plus_copy(i).start()
                share_block(i % 4, (z - 4 + 16) % 16).start()
                minus_arrival(i - 4).wait_recv()
                minus_copy(i).start()
                share_block(i % 4, (z + 4) % 16).start()

        @pl.when(jnp.logical_not(is_src))
        def _():
            plus_arrival(i).wait_recv()
            plus_copy(i).start()
            share_block(i % 4, (z - ahead_from - 4 * (i // 4) + 32) % 16).start()
            minus_arrival(i).wait_recv()
            if i < 4:
                minus_copy(i).start()
            else:
                @pl.when(behind != 3)
                def _():
                    minus_copy(i).start()

            share_block(i % 4, (z + behind_from + 4 * (i // 4)) % 16).start()

    def pump_last():
        @pl.when(is_src)
        def _():
            for i in range(4, 8):
                plus_arrival(i).wait_recv()
                share_block(i % 4, (z + 8) % 16).start()

        other = 1 - c
        for n in range(16):
            b = wbuf.at[n % 4, pl.ds(pl.multiple_of(128 * (2 * (n // 4) + other), 128), 128)]
            remote(b, b, sib_send.at[n], sib_recv.at[n], sibling, h).wait_recv()

    factor = HD ** -0.5 * math.log2(math.e)

    def bias_of(t):
        count = counts_ref[t]
        out = []
        for b in range(KMAX):
            tile = GRID_F * dp - GRID_F + b
            live = jnp.zeros((), jnp.bool_)
            for j in range(KMAX):
                live = live | ((tiles_ref[t, j] == tile) & (j < count))
            out.append(jnp.where(live, 0.0, -DEAD).astype(jnp.float32))
        return out

    def attend(t, hd, bias):
        lanes = slice(hd * HD, hd * HD + HD)
        out_lanes = pl.ds(pl.multiple_of(PAIR * y + HD * hd, HD), HD)
        for part in range(3):
            lo = t * TILE + part * 128
            q = q_rows[lo : lo + 128, lanes]
            scored = [
                lax.dot_general(
                    q, k_ext[b * TILE : (b + 1) * TILE, lanes], (((1,), (1,)), ((), ())),
                    preferred_element_type=jnp.float32,
                )
                for b in range(KMAX)
            ]
            peak = None
            for b in range(KMAX):
                here = jnp.max(scored[b], axis=1, keepdims=True) + bias[b]
                peak = here if peak is None else jnp.maximum(peak, here)
            total, weighted = None, None
            for b in range(KMAX):
                weights = jnp.exp2((scored[b] - (peak - bias[b])) * factor)
                part_sum = jnp.sum(weights, axis=1, keepdims=True)
                part_out = jnp.dot(
                    weights.astype(jnp.bfloat16), v_ext[b * TILE : (b + 1) * TILE, lanes],
                    preferred_element_type=jnp.float32,
                )
                total = part_sum if total is None else total + part_sum
                weighted = part_out if weighted is None else weighted + part_out
            agat[lo : lo + 128, out_lanes] = (weighted / total).astype(jnp.bfloat16)

    def gat_copy(t, hd, i):
        src = agat.at[pl.ds(t * TILE, TILE), pl.ds(pl.multiple_of(PAIR * y + HD * hd, HD), HD)]
        return remote(
            src, src, gat_send.at[2 * t + hd, i], gat_recv.at[2 * t + hd, i], dp, 4 * x + (y + i) % 4
        )

    def gat_arrival(t, hd, i):
        dst = agat.at[pl.ds(t * TILE, TILE), pl.ds(pl.multiple_of(PAIR * ((y + 4 - i) % 4) + HD * hd, HD), HD)]
        return remote(dst, dst, gat_send.at[2 * t + hd, i], gat_recv.at[2 * t + hd, i], dp, h)

    def rs_copy(t, i):
        return remote(
            pc.at[t, i - 1], rc.at[t, i - 1], rs_send.at[t, i - 1], rs_recv.at[t, i - 1], dp, 4 * ((x + i) % 4) + y
        )

    def project(t):
        for i in (2, 1, 3):
            for hd in range(2):
                gat_arrival(t, hd, i).wait_recv()
        rows = agat[t * TILE : (t + 1) * TILE, :]
        for i in (2, 1, 3, 0):
            part = jnp.dot(rows, wbuf[(x + i) % 4], preferred_element_type=jnp.float32)
            if i == 0:
                acc[t] = part
            else:
                pc[t, i - 1] = part.astype(jnp.bfloat16)
                rs_copy(t, i).start()

    def finish(t):
        summed = acc[t]
        for i in (1, 3, 2):
            rs_copy(t, i).wait_recv()
            summed = summed + rc[t, i - 1].astype(jnp.float32)
        out_ref[t * TILE : (t + 1) * TILE, :] = summed.astype(jnp.bfloat16)

    a2a_wait(0)
    halo_start(0)
    pump(0)
    a2a_wait(1)
    halo_start(1)
    pump(1)
    a2a_wait(2)
    pump(2)
    halo_wait_recv(0)
    halo_wait_recv(1)
    for t in range(2):
        bias = bias_of(t)
        for hd in range(2):
            attend(t, hd, bias)
            for i in (2, 1, 3):
                gat_copy(t, hd, i).start()
            pump(3 + 2 * t + hd)
    pump(7)
    pump_last()
    project(0)
    project(1)
    finish(0)
    finish(1)

    @pl.when(jnp.logical_not(is_src))
    def _():
        xr_copy().wait_send()

    for a in range(3):

        def sent_one(i, carry, a=a):
            a2a_copy(a, i).wait_send()
            return carry

        lax.fori_loop(1, 16, sent_one, 0)
    halo_wait_send(0)
    halo_wait_send(1)
    for i in range(8):
        plus_copy(i).wait_send()
        if i < 4:
            minus_copy(i).wait_send()
        else:
            @pl.when(behind != 3)
            def _():
                minus_copy(i).wait_send()
    for n in range(16):
        share(n % 4, 4 * (n // 4), n).wait_send()
    for t in range(2):
        for i in (1, 2, 3):
            for hd in range(2):
                gat_copy(t, hd, i).wait_send()
            rs_copy(t, i).wait_send()


def local(queries, keys, values, key_tiles, key_counts, out_weight):
    dma = pltpu.SemaphoreType.DMA
    vmem = pltpu.VMEM
    bf16 = jnp.bfloat16
    smem_spec = pl.BlockSpec(memory_space=pltpu.SMEM)
    any_spec = pl.BlockSpec(memory_space=pl.ANY)
    return pl.pallas_call(
        kernel,
        out_shape=jax.ShapeDtypeStruct((ROWS, COLS), bf16),
        in_specs=[smem_spec, smem_spec, any_spec, any_spec, any_spec, any_spec],
        out_specs=pl.BlockSpec(memory_space=pltpu.VMEM),
        scratch_shapes=[
            vmem((ROWS, PAIR), bf16),
            vmem((3 * ROWS, PAIR), bf16),
            vmem((3 * ROWS, PAIR), bf16),
            vmem((4, 1024, COLS), bf16),
            vmem((ROWS, 1024), bf16),
            vmem((2, 3, TILE, COLS), bf16),
            vmem((2, 3, TILE, COLS), bf16),
            vmem((2, TILE, COLS), jnp.float32),
            dma((4,)),
            dma((3, 16)), dma((3, 16)),
            dma((2, 2)), dma((2, 2)),
            dma, dma((4,)),
            dma((8,)), dma((8,)),
            dma((8,)), dma((8,)),
            dma((16,)), dma((16,)),
            dma((4, 4)), dma((4, 4)),
            dma((2, 3)), dma((2, 3)),
        ],
        compiler_params=pltpu.CompilerParams(
            collective_id=0, has_side_effects=True, vmem_limit_bytes=56 * 1024 * 1024
        ),
    )(key_tiles, key_counts, queries, keys, values, out_weight)


def solution(mesh):
    in_specs = (
        P(("dp", "head"), None),
        P(("dp", "head"), None),
        P(("dp", "head"), None),
        P("dp", None),
        P("dp"),
        P("dp", "head"),
    )
    out_specs = P("dp", "head")
    return jax.shard_map(local, mesh=mesh, in_specs=in_specs, out_specs=out_specs, check_vma=False)
```

```python
import math

import jax
import jax.numpy as jnp
from jax import lax
from jax.experimental import pallas as pl
from jax.experimental.pallas import tpu as pltpu
from jax.sharding import PartitionSpec as P

HD = 128
TILE = 384
KMAX = 6
GRID_F = 2
ROWS = 768
TOK = 48
PAIR = 256
COLS = 384
DEAD = 1e30
CHUNK = 192
CHUNKS = ROWS // CHUNK
SUBS = 2
SUB = 128 // SUBS
MESH = pl.DeviceIdType.MESH


def kernel(
    tiles_ref, counts_ref, q_hbm, k_hbm, v_hbm, w_hbm, out_ref,
    q_rows, k_ext, v_ext, wbuf, agat, pc, rc, acc,
    local_sem, a2a_send, a2a_recv, halo_send, halo_recv,
    scatter_send, scatter_recv, plus_send, plus_recv, minus_send, minus_recv, sib_send, sib_recv,
    gat_send, gat_recv, rs_send, rs_recv,
):
    dp = lax.axis_index("dp")
    h = lax.axis_index("head")
    z, c = dp // 2, dp % 2
    x, y = h // 4, h % 4
    sibling = dp + 1 - 2 * c

    def remote(src, dst, send, recv, dp_to, h_to):
        return pltpu.make_async_remote_copy(
            src_ref=src, dst_ref=dst, send_sem=send, recv_sem=recv, device_id=(dp_to, h_to), device_id_type=MESH
        )

    def ring_block(zn, core):
        k = (zn - x + 17) % 4
        zs = (zn - k + 17) % 16
        return k, pl.multiple_of(128 * (2 * (zs // 4) + core), 128)

    stays = (z % 4 == x) & (x == 1)
    scatter_dp = 2 * ((z + x + 15) % 16) + c
    scatter_h = 4 * (z % 4) + y
    from_k = (z - x + 17) % 4
    from_dp = 2 * ((z - from_k + 17) % 16) + c

    barrier = pltpu.get_barrier_semaphore()

    def greet(i, carry):
        pl.semaphore_signal(barrier, inc=1, device_id=(dp, (h + i) % 16), device_id_type=MESH)
        return carry

    lax.fori_loop(1, 16, greet, 0)
    for step in (1, 2, 30, 31):
        pl.semaphore_signal(barrier, inc=1, device_id=((dp + step) % 32, h), device_id_type=MESH)

    @pl.when(jnp.logical_not(stays))
    def _():
        pl.semaphore_signal(barrier, inc=1, device_id=(scatter_dp, scatter_h), device_id_type=MESH)
        pl.semaphore_signal(barrier, inc=1, device_id=(from_dp, 4 * from_k + y), device_id_type=MESH)
        pl.semaphore_wait(barrier, 21)

    @pl.when(stays)
    def _():
        pl.semaphore_wait(barrier, 19)

    def scatter_copy():
        dst = wbuf.at[x, pl.ds(pl.multiple_of(128 * (2 * (z // 4) + c), 128), 128)]
        return remote(w_hbm, dst, scatter_send, scatter_recv, scatter_dp, scatter_h)

    first_k, first_row = ring_block(z, c)
    first = wbuf.at[first_k, pl.ds(first_row, 128)]
    w_local = pltpu.make_async_copy(w_hbm, first, local_sem.at[3])

    @pl.when(stays)
    def _():
        w_local.start()

    @pl.when(jnp.logical_not(stays))
    def _():
        scatter_copy().start()

    sources = (k_hbm, v_hbm, q_hbm)
    targets = (k_ext, v_ext, q_rows)
    bases = (ROWS, ROWS, 0)

    def columns_of(head_to):
        return pl.ds(pl.multiple_of(PAIR * (head_to // 4 + 4 * (head_to % 4)), PAIR), PAIR)

    def land(a, head_from):
        return targets[a].at[pl.ds(pl.multiple_of(bases[a] + TOK * head_from, 16), TOK)]

    def a2a_copy(a, i):
        to = (h + i) % 16
        return remote(sources[a].at[:, columns_of(to)], land(a, h), a2a_send.at[a, i], a2a_recv.at[a, i], dp, to)

    def own_copy(a):
        return pltpu.make_async_copy(sources[a].at[:, columns_of(h)], land(a, h), local_sem.at[a])

    for a in range(3):
        own_copy(a).start()

        def start_one(i, carry, a=a):
            a2a_copy(a, i).start()
            return carry

        lax.fori_loop(1, 16, start_one, 0)

    def a2a_wait(a):
        own_copy(a).wait()

        def wait_one(i, carry):
            a2a_copy(a, i).wait_recv()
            return carry

        lax.fori_loop(1, 16, wait_one, 0)

    middle = pl.ds(ROWS, ROWS)
    sides = (pl.ds(0, ROWS), pl.ds(2 * ROWS, ROWS))

    def halo_copy(a, side):
        return remote(
            targets[a].at[middle], targets[a].at[sides[side]], halo_send.at[a, side], halo_recv.at[a, side],
            (dp + 1 + 30 * side) % 32, h,
        )

    has_next, has_prev = dp < 31, dp > 0

    def halo_start(a):
        @pl.when(has_next)
        def _():
            halo_copy(a, 0).start()

        @pl.when(has_prev)
        def _():
            halo_copy(a, 1).start()

    def halo_wait_recv(a):
        @pl.when(has_prev)
        def _():
            halo_copy(a, 0).wait_recv()

        @pl.when(has_next)
        def _():
            halo_copy(a, 1).wait_recv()

    def halo_wait_send(a):
        @pl.when(has_next)
        def _():
            halo_copy(a, 0).wait_send()

        @pl.when(has_prev)
        def _():
            halo_copy(a, 1).wait_send()

    @pl.when(jnp.logical_not(has_prev))
    def _():
        k_ext[0:ROWS, :] = jnp.zeros((ROWS, PAIR), jnp.bfloat16)
        v_ext[0:ROWS, :] = jnp.zeros((ROWS, PAIR), jnp.bfloat16)

    @pl.when(jnp.logical_not(has_next))
    def _():
        k_ext[2 * ROWS : 3 * ROWS, :] = jnp.zeros((ROWS, PAIR), jnp.bfloat16)
        v_ext[2 * ROWS : 3 * ROWS, :] = jnp.zeros((ROWS, PAIR), jnp.bfloat16)

    dp_plus, dp_minus = (dp + 2) % 32, (dp + 30) % 32

    def piece(zn, i, core):
        k, row = ring_block(zn, core)
        return wbuf.at[k, pl.ds(pl.multiple_of(row + SUB * (i % SUBS), SUB), SUB)]

    def plus_copy(i):
        b = piece((z - i // SUBS + 16) % 16, i, c)
        return remote(b, b, plus_send.at[i], plus_recv.at[i], dp_plus, h)

    def plus_arrival(i):
        b = piece((z - 1 - i // SUBS + 16) % 16, i, c)
        return remote(b, b, plus_send.at[i], plus_recv.at[i], dp_plus, h)

    def minus_copy(i):
        b = piece((z + i // SUBS) % 16, i, c)
        return remote(b, b, minus_send.at[i], minus_recv.at[i], dp_minus, h)

    def minus_arrival(i):
        b = piece((z + 1 + i // SUBS) % 16, i, c)
        return remote(b, b, minus_send.at[i], minus_recv.at[i], dp_minus, h)

    def share(zn, i, n):
        b = piece(zn, i, c)
        return remote(b, b, sib_send.at[n], sib_recv.at[n], sibling, h)

    def share_plus(i):
        return share((z - 1 - i // SUBS + 16) % 16, i, SUBS + i)

    def share_minus(i):
        return share((z + 1 + i // SUBS) % 16, i, 9 * SUBS + i)

    def pump(step):
        if step < SUBS:
            if step == 0:
                @pl.when(stays)
                def _():
                    w_local.wait()

                @pl.when(jnp.logical_not(stays))
                def _():
                    remote(first, first, scatter_send, scatter_recv, dp, h).wait_recv()

            plus_copy(step).start()
            minus_copy(step).start()
            share(z, step, step).start()
            return
        i = step - SUBS
        if i >= 8 * SUBS:
            return
        plus_arrival(i).wait_recv()
        if i < 7 * SUBS:
            plus_copy(i + SUBS).start()
        share_plus(i).start()
        if i < 7 * SUBS:
            minus_arrival(i).wait_recv()
            if i < 6 * SUBS:
                minus_copy(i + SUBS).start()
            share_minus(i).start()

    def sibling_wait():
        other = 1 - c
        for n in range(16 * SUBS):
            if n < SUBS:
                zn = z
            elif n < 9 * SUBS:
                zn = (z - n // SUBS + 16) % 16
            else:
                zn = (z + n // SUBS - 8) % 16
            b = piece(zn, n, other)
            remote(b, b, sib_send.at[n], sib_recv.at[n], sibling, h).wait_recv()

    factor = HD ** -0.5 * math.log2(math.e)

    def bias_of(t):
        count = counts_ref[t]
        out = []
        for b in range(KMAX):
            tile = GRID_F * dp - GRID_F + b
            live = jnp.zeros((), jnp.bool_)
            for j in range(KMAX):
                live = live | ((tiles_ref[t, j] == tile) & (j < count))
            out.append(jnp.where(live, 0.0, -DEAD).astype(jnp.float32))
        return out

    def attend(chunk, hd, bias):
        lanes = slice(hd * HD, hd * HD + HD)
        out_lanes = pl.ds(pl.multiple_of(PAIR * y + HD * hd, HD), HD)
        lo = chunk * CHUNK
        q = q_rows[lo : lo + CHUNK, lanes]
        scored = [
            lax.dot_general(
                q, k_ext[b * TILE : (b + 1) * TILE, lanes], (((1,), (1,)), ((), ())),
                preferred_element_type=jnp.float32,
            )
            for b in range(KMAX)
        ]
        peak = None
        for b in range(KMAX):
            here = jnp.max(scored[b], axis=1, keepdims=True) + bias[b]
            peak = here if peak is None else jnp.maximum(peak, here)
        total, weighted = None, None
        for b in range(KMAX):
            weights = jnp.exp2((scored[b] - (peak - bias[b])) * factor)
            part_sum = jnp.sum(weights, axis=1, keepdims=True)
            part_out = jnp.dot(
                weights.astype(jnp.bfloat16), v_ext[b * TILE : (b + 1) * TILE, lanes],
                preferred_element_type=jnp.float32,
            )
            total = part_sum if total is None else total + part_sum
            weighted = part_out if weighted is None else weighted + part_out
        agat[lo : lo + CHUNK, out_lanes] = (weighted / total).astype(jnp.bfloat16)

    def gat_block(chunk, y_of):
        return agat.at[pl.ds(chunk * CHUNK, CHUNK), pl.ds(pl.multiple_of(PAIR * y_of, PAIR), PAIR)]

    def gat_copy(chunk, i):
        b = gat_block(chunk, y)
        return remote(b, b, gat_send.at[chunk, i], gat_recv.at[chunk, i], dp, 4 * x + (y + i) % 4)

    def gat_arrival(chunk, i):
        b = gat_block(chunk, (y + 4 - i) % 4)
        return remote(b, b, gat_send.at[chunk, i], gat_recv.at[chunk, i], dp, h)

    def rs_copy(chunk, i):
        return remote(
            pc.at[chunk, i - 1], rc.at[chunk, i - 1], rs_send.at[chunk, i - 1], rs_recv.at[chunk, i - 1],
            dp, 4 * ((x + i) % 4) + y,
        )

    def project(chunk):
        for i in (1, 3, 2):
            gat_arrival(chunk, i).wait_recv()
        rows = agat[chunk * CHUNK : (chunk + 1) * CHUNK, :]
        for i in (2, 1, 3, 0):
            part = jnp.dot(rows, wbuf[(x + i) % 4], preferred_element_type=jnp.float32)
            if i == 0:
                acc[chunk] = part
            else:
                pc[chunk, i - 1] = part.astype(jnp.bfloat16)
                rs_copy(chunk, i).start()

    def finish(chunk):
        summed = acc[chunk]
        for i in (1, 3, 2):
            rs_copy(chunk, i).wait_recv()
            summed = summed + rc[chunk, i - 1].astype(jnp.float32)
        out_ref[chunk * CHUNK : (chunk + 1) * CHUNK, :] = summed.astype(jnp.bfloat16)

    biases = [bias_of(0), bias_of(1)]

    def attention(chunk, pumps):
        for hd in range(2):
            attend(chunk, hd, biases[chunk * CHUNK // TILE])
            for step in pumps[hd]:
                pump(step)
        for i in (2, 1, 3):
            gat_copy(chunk, i).start()

    pump(0)
    pump(1)
    a2a_wait(0)
    halo_start(0)
    pump(2)
    pump(3)
    a2a_wait(1)
    halo_start(1)
    for step in (4, 5, 6, 7):
        pump(step)
    a2a_wait(2)
    pump(8)
    pump(9)
    halo_wait_recv(0)
    halo_wait_recv(1)
    attention(0, ((10, 11), (12, 13)))
    attention(1, ((14, 15), (16, 17)))
    sibling_wait()
    project(0)
    attention(2, ((), ()))
    project(1)
    attention(3, ((), ()))
    project(2)
    project(3)
    for chunk in range(CHUNKS):
        finish(chunk)

    @pl.when(jnp.logical_not(stays))
    def _():
        scatter_copy().wait_send()

    for a in range(3):

        def sent_one(i, carry, a=a):
            a2a_copy(a, i).wait_send()
            return carry

        lax.fori_loop(1, 16, sent_one, 0)
    halo_wait_send(0)
    halo_wait_send(1)
    for i in range(8 * SUBS):
        plus_copy(i).wait_send()
        share_plus(i).wait_send()
        if i < 7 * SUBS:
            minus_copy(i).wait_send()
            share_minus(i).wait_send()
    for i in range(SUBS):
        share(z, i, i).wait_send()
    for chunk in range(CHUNKS):
        for i in (1, 2, 3):
            gat_copy(chunk, i).wait_send()
            rs_copy(chunk, i).wait_send()


def local(queries, keys, values, key_tiles, key_counts, out_weight):
    dma = pltpu.SemaphoreType.DMA
    vmem = pltpu.VMEM
    bf16 = jnp.bfloat16
    smem_spec = pl.BlockSpec(memory_space=pltpu.SMEM)
    any_spec = pl.BlockSpec(memory_space=pl.ANY)
    return pl.pallas_call(
        kernel,
        out_shape=jax.ShapeDtypeStruct((ROWS, COLS), bf16),
        in_specs=[smem_spec, smem_spec, any_spec, any_spec, any_spec, any_spec],
        out_specs=pl.BlockSpec(memory_space=pltpu.VMEM),
        scratch_shapes=[
            vmem((ROWS, PAIR), bf16),
            vmem((3 * ROWS, PAIR), bf16),
            vmem((3 * ROWS, PAIR), bf16),
            vmem((4, 1024, COLS), bf16),
            vmem((ROWS, 1024), bf16),
            vmem((CHUNKS, 3, CHUNK, COLS), bf16),
            vmem((CHUNKS, 3, CHUNK, COLS), bf16),
            vmem((CHUNKS, CHUNK, COLS), jnp.float32),
            dma((4,)),
            dma((3, 16)), dma((3, 16)),
            dma((2, 2)), dma((2, 2)),
            dma, dma,
            dma((8 * SUBS,)), dma((8 * SUBS,)),
            dma((7 * SUBS,)), dma((7 * SUBS,)),
            dma((16 * SUBS,)), dma((16 * SUBS,)),
            dma((CHUNKS, 4)), dma((CHUNKS, 4)),
            dma((CHUNKS, 3)), dma((CHUNKS, 3)),
        ],
        compiler_params=pltpu.CompilerParams(
            collective_id=0, has_side_effects=True, vmem_limit_bytes=56 * 1024 * 1024
        ),
    )(key_tiles, key_counts, queries, keys, values, out_weight)


def solution(mesh):
    in_specs = (
        P(("dp", "head"), None),
        P(("dp", "head"), None),
        P(("dp", "head"), None),
        P("dp", None),
        P("dp"),
        P("dp", "head"),
    )
    out_specs = P("dp", "head")
    return jax.shard_map(local, mesh=mesh, in_specs=in_specs, out_specs=out_specs, check_vma=False)
```

```python
import math

import jax
import jax.numpy as jnp
from jax import lax
from jax.experimental import pallas as pl
from jax.experimental.pallas import tpu as pltpu
from jax.sharding import PartitionSpec as P

HD = 128
TILE = 384
KMAX = 6
GRID_F = 2
ROWS = 768
TOK = 48
PAIR = 256
COLS = 384
DEAD = 1e30
CHUNK = 192
CHUNKS = ROWS // CHUNK
MESH = pl.DeviceIdType.MESH


def kernel(
    tiles_ref, counts_ref, q_hbm, k_hbm, v_hbm, w_hbm, out_ref,
    q_rows, k_ext, v_ext, wbuf, agat, pc, rc, acc,
    local_sem, a2a_send, a2a_recv, halo_send, halo_recv,
    scatter_send, scatter_recv, plus_send, plus_recv, minus_send, minus_recv, up_send, up_recv, down_send, down_recv, sib_send, sib_recv,
    gat_send, gat_recv, rs_send, rs_recv,
):
    dp = lax.axis_index("dp")
    h = lax.axis_index("head")
    z, c = dp // 2, dp % 2
    x, y = h // 4, h % 4
    sibling = dp + 1 - 2 * c

    def remote(src, dst, send, recv, dp_to, h_to):
        return pltpu.make_async_remote_copy(
            src_ref=src, dst_ref=dst, send_sem=send, recv_sem=recv, device_id=(dp_to, h_to), device_id_type=MESH
        )

    def ring_block(zn, core):
        k = (zn - x + 17) % 4
        zs = (zn - k + 17) % 16
        return k, pl.multiple_of(128 * (2 * (zs // 4) + core), 128)

    stays = (z % 4 == x) & (x == 1)
    scatter_dp = 2 * ((z + x + 15) % 16) + c
    scatter_h = 4 * (z % 4) + y
    from_k = (z - x + 17) % 4
    from_dp = 2 * ((z - from_k + 17) % 16) + c

    barrier = pltpu.get_barrier_semaphore()

    def greet(i, carry):
        pl.semaphore_signal(barrier, inc=1, device_id=(dp, (h + i) % 16), device_id_type=MESH)
        return carry

    lax.fori_loop(1, 16, greet, 0)
    for step in (1, 2, 4, 28, 30, 31):
        pl.semaphore_signal(barrier, inc=1, device_id=((dp + step) % 32, h), device_id_type=MESH)

    @pl.when(jnp.logical_not(stays))
    def _():
        pl.semaphore_signal(barrier, inc=1, device_id=(scatter_dp, scatter_h), device_id_type=MESH)
        pl.semaphore_signal(barrier, inc=1, device_id=(from_dp, 4 * from_k + y), device_id_type=MESH)
        pl.semaphore_wait(barrier, 23)

    @pl.when(stays)
    def _():
        pl.semaphore_wait(barrier, 21)

    def scatter_copy():
        dst = wbuf.at[x, pl.ds(pl.multiple_of(128 * (2 * (z // 4) + c), 128), 128)]
        return remote(w_hbm, dst, scatter_send, scatter_recv, scatter_dp, scatter_h)

    first_k, first_row = ring_block(z, c)
    first = wbuf.at[first_k, pl.ds(first_row, 128)]
    w_local = pltpu.make_async_copy(w_hbm, first, local_sem.at[3])

    @pl.when(stays)
    def _():
        w_local.start()

    @pl.when(jnp.logical_not(stays))
    def _():
        scatter_copy().start()

    sources = (k_hbm, v_hbm, q_hbm)
    targets = (k_ext, v_ext, q_rows)
    bases = (ROWS, ROWS, 0)

    def columns_of(head_to):
        return pl.ds(pl.multiple_of(PAIR * (head_to // 4 + 4 * (head_to % 4)), PAIR), PAIR)

    def land(a, head_from):
        return targets[a].at[pl.ds(pl.multiple_of(bases[a] + TOK * head_from, 16), TOK)]

    def a2a_copy(a, i):
        to = (h + i) % 16
        return remote(sources[a].at[:, columns_of(to)], land(a, h), a2a_send.at[a, i], a2a_recv.at[a, i], dp, to)

    def own_copy(a):
        return pltpu.make_async_copy(sources[a].at[:, columns_of(h)], land(a, h), local_sem.at[a])

    for a in range(3):
        own_copy(a).start()

        def start_one(i, carry, a=a):
            a2a_copy(a, i).start()
            return carry

        lax.fori_loop(1, 16, start_one, 0)

    def a2a_wait(a):
        own_copy(a).wait()

        def wait_one(i, carry):
            a2a_copy(a, i).wait_recv()
            return carry

        lax.fori_loop(1, 16, wait_one, 0)

    middle = pl.ds(ROWS, ROWS)
    sides = (pl.ds(0, ROWS), pl.ds(2 * ROWS, ROWS))

    def halo_copy(a, side):
        return remote(
            targets[a].at[middle], targets[a].at[sides[side]], halo_send.at[a, side], halo_recv.at[a, side],
            (dp + 1 + 30 * side) % 32, h,
        )

    has_next, has_prev = dp < 31, dp > 0

    def halo_start(a):
        @pl.when(has_next)
        def _():
            halo_copy(a, 0).start()

        @pl.when(has_prev)
        def _():
            halo_copy(a, 1).start()

    def halo_wait_recv(a):
        @pl.when(has_prev)
        def _():
            halo_copy(a, 0).wait_recv()

        @pl.when(has_next)
        def _():
            halo_copy(a, 1).wait_recv()

    def halo_wait_send(a):
        @pl.when(has_next)
        def _():
            halo_copy(a, 0).wait_send()

        @pl.when(has_prev)
        def _():
            halo_copy(a, 1).wait_send()

    @pl.when(jnp.logical_not(has_prev))
    def _():
        k_ext[0:ROWS, :] = jnp.zeros((ROWS, PAIR), jnp.bfloat16)
        v_ext[0:ROWS, :] = jnp.zeros((ROWS, PAIR), jnp.bfloat16)

    @pl.when(jnp.logical_not(has_next))
    def _():
        k_ext[2 * ROWS : 3 * ROWS, :] = jnp.zeros((ROWS, PAIR), jnp.bfloat16)
        v_ext[2 * ROWS : 3 * ROWS, :] = jnp.zeros((ROWS, PAIR), jnp.bfloat16)

    def piece(offset, core):
        k, row = ring_block((z + offset + 16) % 16, core)
        return wbuf.at[k, pl.ds(row, 128)]

    def along(offset, sends, recvs, n, step):
        b = piece(offset, c)
        return remote(b, b, sends.at[n], recvs.at[n], (dp + 2 * step + 32) % 32, h)

    def plus_copy(n):
        return along(-2 * n, plus_send, plus_recv, n, 2)

    def minus_copy(n):
        return along(2 * n, minus_send, minus_recv, n, -2)

    def up_copy(n):
        return along(-2 * n, up_send, up_recv, n, 1)

    def down_copy(n):
        return along(2 * n, down_send, down_recv, n, -1)

    def share(offset):
        b = piece(offset, c)
        n = (offset + 16) % 16
        return remote(b, b, sib_send.at[n], sib_recv.at[n], sibling, h)

    def ring_start():
        @pl.when(stays)
        def _():
            w_local.wait()

        @pl.when(jnp.logical_not(stays))
        def _():
            remote(first, first, scatter_send, scatter_recv, dp, h).wait_recv()

        plus_copy(0).start()
        minus_copy(0).start()
        share(0).start()

    def ring_step(n):
        along(-2 * (n + 1), plus_send, plus_recv, n, 2).wait_recv()
        if n < 3:
            plus_copy(n + 1).start()
        share(-2 * (n + 1)).start()
        if n < 3:
            along(2 * (n + 1), minus_send, minus_recv, n, -2).wait_recv()
            if n < 2:
                minus_copy(n + 1).start()
            share(2 * (n + 1)).start()

    def hand_on(n):
        up_copy(n).start()
        down_copy(n).start()

    def handed(n):
        along(-1 - 2 * n, up_send, up_recv, n, 1).wait_recv()
        share(-1 - 2 * n).start()
        along(1 + 2 * n, down_send, down_recv, n, -1).wait_recv()
        share(1 + 2 * n).start()

    def sibling_wait(odd):
        for n in range(odd, 16, 2):
            b = piece(n, 1 - c)
            remote(b, b, sib_send.at[n], sib_recv.at[n], sibling, h).wait_recv()

    factor = HD ** -0.5 * math.log2(math.e)

    def bias_of(t):
        count = counts_ref[t]
        out = []
        for b in range(KMAX):
            tile = GRID_F * dp - GRID_F + b
            live = jnp.zeros((), jnp.bool_)
            for j in range(KMAX):
                live = live | ((tiles_ref[t, j] == tile) & (j < count))
            out.append(jnp.where(live, 0.0, -DEAD).astype(jnp.float32))
        return out

    def attend(chunk, hd, bias):
        lanes = slice(hd * HD, hd * HD + HD)
        out_lanes = pl.ds(pl.multiple_of(PAIR * y + HD * hd, HD), HD)
        lo = chunk * CHUNK
        q = q_rows[lo : lo + CHUNK, lanes]
        scored = [
            lax.dot_general(
                q, k_ext[b * TILE : (b + 1) * TILE, lanes], (((1,), (1,)), ((), ())),
                preferred_element_type=jnp.float32,
            )
            for b in range(KMAX)
        ]
        peak = None
        for b in range(KMAX):
            here = jnp.max(scored[b], axis=1, keepdims=True) + bias[b]
            peak = here if peak is None else jnp.maximum(peak, here)
        total, weighted = None, None
        for b in range(KMAX):
            weights = jnp.exp2((scored[b] - (peak - bias[b])) * factor)
            part_sum = jnp.sum(weights, axis=1, keepdims=True)
            part_out = jnp.dot(
                weights.astype(jnp.bfloat16), v_ext[b * TILE : (b + 1) * TILE, lanes],
                preferred_element_type=jnp.float32,
            )
            total = part_sum if total is None else total + part_sum
            weighted = part_out if weighted is None else weighted + part_out
        agat[lo : lo + CHUNK, out_lanes] = (weighted / total).astype(jnp.bfloat16)

    def gat_block(chunk, y_of):
        return agat.at[pl.ds(chunk * CHUNK, CHUNK), pl.ds(pl.multiple_of(PAIR * y_of, PAIR), PAIR)]

    def gat_copy(chunk, i):
        b = gat_block(chunk, y)
        return remote(b, b, gat_send.at[chunk, i], gat_recv.at[chunk, i], dp, 4 * x + (y + i) % 4)

    def gat_arrival(chunk, i):
        b = gat_block(chunk, (y + 4 - i) % 4)
        return remote(b, b, gat_send.at[chunk, i], gat_recv.at[chunk, i], dp, h)

    first_way = (z + 1) % 2

    def rs_copy(chunk, i):
        return remote(
            pc.at[chunk, i - 1], rc.at[chunk, i - 1], rs_send.at[chunk, i - 1], rs_recv.at[chunk, i - 1],
            dp, 4 * ((x + i) % 4) + y,
        )

    def gathered(chunk):
        for i in (1, 3, 2):
            gat_arrival(chunk, i).wait_recv()

    def project(chunk, late):
        rows = agat[chunk * CHUNK : (chunk + 1) * CHUNK, :]
        way = first_way + late * (1 - 2 * first_way)
        for i in (way + 2, way):
            part = jnp.dot(rows, wbuf[(x + i) % 4], preferred_element_type=jnp.float32)

            @pl.when(i == 0)
            def _():
                acc[chunk] = part

            @pl.when(i > 0)
            def _():
                pc[chunk, i - 1] = part.astype(jnp.bfloat16)
                rs_copy(chunk, i).start()

    def finish(chunk):
        summed = acc[chunk]
        for i in (1, 3, 2):
            rs_copy(chunk, i).wait_recv()
            summed = summed + rc[chunk, i - 1].astype(jnp.float32)
        out_ref[chunk * CHUNK : (chunk + 1) * CHUNK, :] = summed.astype(jnp.bfloat16)

    biases = [bias_of(0), bias_of(1)]

    def attention(chunk):
        for hd in range(2):
            attend(chunk, hd, biases[chunk * CHUNK // TILE])
        for i in (2, 1, 3):
            gat_copy(chunk, i).start()

    ring_start()
    a2a_wait(0)
    halo_start(0)
    ring_step(0)
    a2a_wait(1)
    halo_start(1)
    ring_step(1)
    a2a_wait(2)
    halo_wait_recv(0)
    halo_wait_recv(1)
    attention(0)
    attention(1)
    ring_step(2)
    attention(2)
    attention(3)
    hand_on(0)
    hand_on(1)
    hand_on(2)
    ring_step(3)
    hand_on(3)
    sibling_wait(0)
    gathered(0)
    project(0, 0)
    gathered(1)
    project(1, 0)
    gathered(2)
    project(2, 0)
    gathered(3)
    project(3, 0)
    handed(0)
    handed(1)
    handed(2)
    handed(3)
    sibling_wait(1)
    project(0, 1)
    project(1, 1)
    project(2, 1)
    project(3, 1)

    @pl.when(jnp.logical_not(stays))
    def _():
        scatter_copy().wait_send()

    for a in range(3):

        def sent_one(i, carry, a=a):
            a2a_copy(a, i).wait_send()
            return carry

        lax.fori_loop(1, 16, sent_one, 0)
    halo_wait_send(0)
    halo_wait_send(1)
    for n in range(4):
        plus_copy(n).wait_send()
        if n < 3:
            minus_copy(n).wait_send()
        up_copy(n).wait_send()
        down_copy(n).wait_send()
    for n in range(16):
        share(n).wait_send()
    for chunk in range(CHUNKS):
        for i in (1, 2, 3):
            gat_copy(chunk, i).wait_send()

    for chunk in range(CHUNKS):
        finish(chunk)

    for chunk in range(CHUNKS):
        for i in (1, 2, 3):
            rs_copy(chunk, i).wait_send()


def local(queries, keys, values, key_tiles, key_counts, out_weight):
    dma = pltpu.SemaphoreType.DMA
    vmem = pltpu.VMEM
    bf16 = jnp.bfloat16
    smem_spec = pl.BlockSpec(memory_space=pltpu.SMEM)
    any_spec = pl.BlockSpec(memory_space=pl.ANY)
    return pl.pallas_call(
        kernel,
        out_shape=jax.ShapeDtypeStruct((ROWS, COLS), bf16),
        in_specs=[smem_spec, smem_spec, any_spec, any_spec, any_spec, any_spec],
        out_specs=pl.BlockSpec(memory_space=pltpu.VMEM),
        scratch_shapes=[
            vmem((ROWS, PAIR), bf16),
            vmem((3 * ROWS, PAIR), bf16),
            vmem((3 * ROWS, PAIR), bf16),
            vmem((4, 1024, COLS), bf16),
            vmem((ROWS, 1024), bf16),
            vmem((CHUNKS, 3, CHUNK, COLS), bf16),
            vmem((CHUNKS, 3, CHUNK, COLS), bf16),
            vmem((CHUNKS, CHUNK, COLS), jnp.float32),
            dma((4,)),
            dma((3, 16)), dma((3, 16)),
            dma((2, 2)), dma((2, 2)),
            dma, dma,
            dma((4,)), dma((4,)),
            dma((3,)), dma((3,)),
            dma((4,)), dma((4,)),
            dma((4,)), dma((4,)),
            dma((16,)), dma((16,)),
            dma((CHUNKS, 4)), dma((CHUNKS, 4)),
            dma((CHUNKS, 3)), dma((CHUNKS, 3)),
        ],
        compiler_params=pltpu.CompilerParams(
            collective_id=0, has_side_effects=True, vmem_limit_bytes=56 * 1024 * 1024
        ),
    )(key_tiles, key_counts, queries, keys, values, out_weight)


def solution(mesh):
    in_specs = (
        P(("dp", "head"), None),
        P(("dp", "head"), None),
        P(("dp", "head"), None),
        P("dp", None),
        P("dp"),
        P("dp", "head"),
    )
    out_specs = P("dp", "head")
    return jax.shard_map(local, mesh=mesh, in_specs=in_specs, out_specs=out_specs, check_vma=False)
```

```python
import math

import jax
import jax.numpy as jnp
from jax import lax
from jax.experimental import pallas as pl
from jax.experimental.pallas import tpu as pltpu
from jax.sharding import PartitionSpec as P

HD = 128
TILE = 384
KMAX = 6
GRID_F = 2
ROWS = 768
TOK = 48
PAIR = 256
COLS = 384
DEAD = 1e30
CHUNK = 192
CHUNKS = ROWS // CHUNK
MESH = pl.DeviceIdType.MESH


def kernel(
    tiles_ref, counts_ref, q_hbm, k_hbm, v_hbm, w_hbm, out_ref,
    q_rows, k_ext, v_ext, weight, agat,
    local_sem, a2a_send, a2a_recv, halo_send, halo_recv, known,
    far_send, far_recv, half_send, half_recv, near_send, near_recv, next_send, next_recv, sib_send, sib_recv,
    s1_send, s1_recv, s2_send, s2_recv, s3_send, s3_recv,
):
    dp = lax.axis_index("dp")
    h = lax.axis_index("head")
    z, c = dp // 2, dp % 2
    x, y = h // 4, h % 4
    sibling = dp + 1 - 2 * c

    def remote(src, dst, send, recv, dp_to, h_to):
        return pltpu.make_async_remote_copy(
            src_ref=src, dst_ref=dst, send_sem=send, recv_sem=recv, device_id=(dp_to, h_to), device_id_type=MESH
        )

    has_next, has_prev = dp < 31, dp > 0
    has_up, has_down = z < 15, z > 0
    barrier = pltpu.get_barrier_semaphore()

    def signal(sem, dp_to, h_to):
        pl.semaphore_signal(sem, inc=1, device_id=(dp_to, h_to), device_id_type=MESH)

    def greet(i, carry):
        signal(barrier, dp, (h + i) % 16)
        return carry

    lax.fori_loop(1, 16, greet, 0)
    for there, step in ((has_next, 1), (has_prev, -1), (has_up, 2), (has_down, -2)):
        @pl.when(there)
        def _():
            signal(barrier, (dp + step + 32) % 32, h)

    @pl.when(has_up & has_down)
    def _():
        pl.semaphore_wait(barrier, 19)

    @pl.when(jnp.logical_not(has_up) | jnp.logical_not(has_down))
    def _():
        @pl.when(has_next & has_prev)
        def _():
            pl.semaphore_wait(barrier, 18)

        @pl.when(jnp.logical_not(has_next) | jnp.logical_not(has_prev))
        def _():
            pl.semaphore_wait(barrier, 17)

    def meet_signal(r):
        @pl.when(z + 2**r < 16)
        def _():
            signal(known.at[r, 0], (dp + 2 ** (r + 1)) % 32, h)

        @pl.when(z >= 2**r)
        def _():
            signal(known.at[r, 1], (dp - 2 ** (r + 1) + 32) % 32, h)

    def meet_wait(r):
        @pl.when(z >= 2**r)
        def _():
            pl.semaphore_wait(known.at[r, 0], 1)

        @pl.when(z + 2**r < 16)
        def _():
            pl.semaphore_wait(known.at[r, 1], 1)

    meet_signal(0)

    sources = (k_hbm, v_hbm, q_hbm)
    targets = (k_ext, v_ext, q_rows)
    bases = (ROWS, ROWS, 0)

    def columns_of(head_to):
        return pl.ds(pl.multiple_of(PAIR * head_to, PAIR), PAIR)

    def land(a, head_from):
        return targets[a].at[pl.ds(pl.multiple_of(bases[a] + TOK * head_from, 16), TOK)]

    def a2a_copy(a, i):
        to = (h + i) % 16
        return remote(sources[a].at[:, columns_of(to)], land(a, h), a2a_send.at[a, i], a2a_recv.at[a, i], dp, to)

    def own_copy(a):
        return pltpu.make_async_copy(sources[a].at[:, columns_of(h)], land(a, h), local_sem.at[a])

    for a in range(3):
        own_copy(a).start()

        def start_one(i, carry, a=a):
            a2a_copy(a, i).start()
            return carry

        lax.fori_loop(1, 16, start_one, 0)

    def a2a_wait(a):
        own_copy(a).wait()

        def wait_one(i, carry):
            a2a_copy(a, i).wait_recv()
            return carry

        lax.fori_loop(1, 16, wait_one, 0)

    middle = pl.ds(ROWS, ROWS)
    sides = (pl.ds(0, ROWS), pl.ds(2 * ROWS, ROWS))

    def halo_copy(a, side):
        return remote(
            targets[a].at[middle], targets[a].at[sides[side]], halo_send.at[a, side], halo_recv.at[a, side],
            (dp + 1 + 30 * side) % 32, h,
        )

    def halo_start(a):
        @pl.when(has_next)
        def _():
            halo_copy(a, 0).start()

        @pl.when(has_prev)
        def _():
            halo_copy(a, 1).start()

    def halo_wait_recv(a):
        @pl.when(has_prev)
        def _():
            halo_copy(a, 0).wait_recv()

        @pl.when(has_next)
        def _():
            halo_copy(a, 1).wait_recv()

    def halo_wait_send(a):
        @pl.when(has_next)
        def _():
            halo_copy(a, 0).wait_send()

        @pl.when(has_prev)
        def _():
            halo_copy(a, 1).wait_send()

    @pl.when(jnp.logical_not(has_prev))
    def _():
        k_ext[0:ROWS, :] = jnp.zeros((ROWS, PAIR), jnp.bfloat16)
        v_ext[0:ROWS, :] = jnp.zeros((ROWS, PAIR), jnp.bfloat16)

    @pl.when(jnp.logical_not(has_next))
    def _():
        k_ext[2 * ROWS : 3 * ROWS, :] = jnp.zeros((ROWS, PAIR), jnp.bfloat16)
        v_ext[2 * ROWS : 3 * ROWS, :] = jnp.zeros((ROWS, PAIR), jnp.bfloat16)

    def weight_block(offset, core, first=0, count=128):
        return weight.at[core, pl.ds(pl.multiple_of(128 * ((z + offset + 16) % 16) + first, 64), count)]

    def along(offset, step, sends, recvs, first=0, count=128):
        b = weight_block(offset, c, first, count)
        return remote(b, b, sends, recvs, (dp + 2 * step + 32) % 32, h)

    w_local = pltpu.make_async_copy(w_hbm, weight_block(0, c), local_sem.at[3])
    w_local.start()

    def far_copy(side):
        return along(0, 4 - 8 * side, far_send.at[side], far_recv.at[side])

    def far_arrival(side):
        return along(8 * side - 4, 4 - 8 * side, far_send.at[side], far_recv.at[side])

    def far_start(wraps):
        for side, inside in ((0, z < 12), (1, z >= 4)):
            @pl.when(jnp.logical_not(inside) if wraps else inside)
            def _():
                far_copy(side).start()

    def half_copy(side):
        return along(8 * side - 4, 4 - 8 * side, half_send.at[side], half_recv.at[side], 64 * side, 64)

    def half_arrival(side):
        return along(8, 4 - 8 * side, half_send.at[side], half_recv.at[side], 64 * side, 64)

    def near_copy(m, side):
        return along(4 * m, 1 - 2 * side, near_send.at[side, m], near_recv.at[side, m])

    def near_arrival(m, side):
        return along((4 * m + 15 + 2 * side) % 16, 1 - 2 * side, near_send.at[side, m], near_recv.at[side, m])

    def next_copy(m, side):
        return along((4 * m + 15 + 2 * side) % 16, 1 - 2 * side, next_send.at[side, m], next_recv.at[side, m])

    def next_arrival(m, side):
        return along((4 * m + 14 + 4 * side) % 16, 1 - 2 * side, next_send.at[side, m], next_recv.at[side, m])

    PASSED = ((0, 3), (0, 1))

    def share(offset):
        b = weight_block(offset, c)
        return remote(b, b, sib_send.at[offset], sib_recv.at[offset], sibling, h)

    def far_pass():
        for side in range(2):
            far_arrival(side).wait_recv()
            half_copy(side).start()
        for m in (0, 3, 1):
            for side in range(2):
                near_copy(m, side).start()
        share(12).start()
        share(4).start()

    def half_pass():
        for side in range(2):
            half_arrival(side).wait_recv()
        for side in range(2):
            near_copy(2, side).start()
        share(8).start()

    def near_pass():
        for m in (0, 3, 1, 2):
            for side in range(2):
                near_arrival(m, side).wait_recv()
                if m in PASSED[side]:
                    next_copy(m, side).start()
                share((4 * m + 15 + 2 * side) % 16).start()

    def next_done():
        for side in range(2):
            for m in PASSED[side]:
                next_arrival(m, side).wait_recv()
                share((4 * m + 14 + 4 * side) % 16).start()

    def sibling_done():
        for offset in range(16):
            b = weight_block(offset, 1 - c)
            remote(b, b, sib_send.at[offset], sib_recv.at[offset], sibling, h).wait_recv()

    factor = HD ** -0.5 * math.log2(math.e)

    def bias_of(t):
        count = counts_ref[t]
        out = []
        for b in range(KMAX):
            tile = GRID_F * dp - GRID_F + b
            live = jnp.zeros((), jnp.bool_)
            for j in range(KMAX):
                live = live | ((tiles_ref[t, j] == tile) & (j < count))
            out.append(jnp.where(live, 0.0, -DEAD).astype(jnp.float32))
        return out

    def attend(chunk, hd, bias):
        lanes = slice(hd * HD, hd * HD + HD)
        out_lanes = pl.ds(pl.multiple_of(HD * h, HD), HD)
        lo = chunk * CHUNK
        q = q_rows[lo : lo + CHUNK, lanes]
        scored = [
            lax.dot_general(
                q, k_ext[b * TILE : (b + 1) * TILE, lanes], (((1,), (1,)), ((), ())),
                preferred_element_type=jnp.float32,
            )
            for b in range(KMAX)
        ]
        peak = None
        for b in range(KMAX):
            here = jnp.max(scored[b], axis=1, keepdims=True) + bias[b]
            peak = here if peak is None else jnp.maximum(peak, here)
        total, weighted = None, None
        for b in range(KMAX):
            weights = jnp.exp2((scored[b] - (peak - bias[b])) * factor)
            part_sum = jnp.sum(weights, axis=1, keepdims=True)
            part_out = jnp.dot(
                weights.astype(jnp.bfloat16), v_ext[b * TILE : (b + 1) * TILE, lanes],
                preferred_element_type=jnp.float32,
            )
            total = part_sum if total is None else total + part_sum
            weighted = part_out if weighted is None else weighted + part_out
        agat[hd, lo : lo + CHUNK, out_lanes] = (weighted / total).astype(jnp.bfloat16)

    def place(chunk, i, steps):
        if chunk % 2 == 0:
            return 4 * ((x + steps + 4) % 4) + (y - i + 4) % 4
        return 4 * ((x - i + 4) % 4) + (y + steps + 4) % 4

    def gathered_block(chunk, u):
        return agat.at[:, pl.ds(chunk * CHUNK, CHUNK), pl.ds(pl.multiple_of(HD * u, HD), HD)]

    def hop(chunk, u, to, sends, recvs):
        b = gathered_block(chunk, u)
        return remote(b, b, sends, recvs, dp, to)

    def first_copy(chunk, i):
        return hop(chunk, h, place(chunk, -i, 0), s1_send.at[chunk, i], s1_recv.at[chunk, i])

    def first_arrival(chunk, i):
        return hop(chunk, place(chunk, i, 0), h, s1_send.at[chunk, i], s1_recv.at[chunk, i])

    def second_copy(chunk, i, side):
        return hop(
            chunk, place(chunk, i, 0), place(chunk, 0, 1 - 2 * side),
            s2_send.at[chunk, side, i], s2_recv.at[chunk, side, i],
        )

    def second_arrival(chunk, i, side):
        return hop(
            chunk, place(chunk, i, 2 * side - 1), h, s2_send.at[chunk, side, i], s2_recv.at[chunk, side, i]
        )

    def third_copy(chunk, n, side):
        return hop(
            chunk, place(chunk, n + 2 * side, 2 * side - 1), place(chunk, 0, 1 - 2 * side),
            s3_send.at[chunk, side, n], s3_recv.at[chunk, side, n],
        )

    def third_arrival(chunk, n, side):
        return hop(
            chunk, place(chunk, n + 2 * side, 2), h, s3_send.at[chunk, side, n], s3_recv.at[chunk, side, n]
        )

    def send_first(chunk):
        for i in (2, 1, 3):
            first_copy(chunk, i).start()
        for side in range(2):
            second_copy(chunk, 0, side).start()

    def send_second(chunk):
        for i in (1, 3, 2):
            first_arrival(chunk, i).wait_recv()
            for side in range(2):
                second_copy(chunk, i, side).start()

    def send_third(chunk):
        for i in (0, 1, 3, 2):
            for side in range(2):
                second_arrival(chunk, i, side).wait_recv()
                if i // 2 == side:
                    third_copy(chunk, i % 2, side).start()

    def last_arrivals(chunk):
        for n in range(2):
            for side in range(2):
                third_arrival(chunk, n, side).wait_recv()

    def project(chunk):
        rows = slice(chunk * CHUNK, (chunk + 1) * CHUNK)
        out = None
        for part in range(2):
            term = jnp.dot(agat[part, rows, :], weight[part], preferred_element_type=jnp.float32)
            out = term if out is None else out + term
        out_ref[rows, :] = out.astype(jnp.bfloat16)

    biases = [bias_of(0), bias_of(1)]

    def attention(chunk):
        for hd in range(2):
            attend(chunk, hd, biases[chunk * CHUNK // TILE])
        send_first(chunk)

    meet_wait(0)
    meet_signal(1)
    a2a_wait(0)
    halo_start(0)
    meet_wait(1)
    meet_signal(2)
    a2a_wait(1)
    halo_start(1)
    w_local.wait()
    share(0).start()
    far_start(False)
    meet_wait(2)
    meet_signal(3)
    a2a_wait(2)
    meet_wait(3)
    far_start(True)
    halo_wait_recv(0)
    halo_wait_recv(1)
    attention(0)
    attention(1)
    send_second(0)
    attention(2)
    far_pass()
    attention(3)
    send_second(1)
    half_pass()
    send_third(0)
    send_second(2)
    send_third(1)
    send_second(3)
    near_pass()
    send_third(2)
    last_arrivals(0)
    send_third(3)
    last_arrivals(1)
    next_done()
    sibling_done()
    project(0)
    project(1)
    last_arrivals(2)
    project(2)
    last_arrivals(3)
    project(3)

    for a in range(3):

        def sent_one(i, carry, a=a):
            a2a_copy(a, i).wait_send()
            return carry

        lax.fori_loop(1, 16, sent_one, 0)
    halo_wait_send(0)
    halo_wait_send(1)
    for side in range(2):
        far_copy(side).wait_send()
        half_copy(side).wait_send()
        for m in range(4):
            near_copy(m, side).wait_send()
        for m in PASSED[side]:
            next_copy(m, side).wait_send()
    for offset in range(16):
        share(offset).wait_send()
    for chunk in range(CHUNKS):
        for i in range(4):
            if i > 0:
                first_copy(chunk, i).wait_send()
            for side in range(2):
                second_copy(chunk, i, side).wait_send()
                if i < 2:
                    third_copy(chunk, i, side).wait_send()


def local(queries, keys, values, key_tiles, key_counts, out_weight):
    dma = pltpu.SemaphoreType.DMA
    vmem = pltpu.VMEM
    bf16 = jnp.bfloat16
    smem_spec = pl.BlockSpec(memory_space=pltpu.SMEM)
    any_spec = pl.BlockSpec(memory_space=pl.ANY)
    return pl.pallas_call(
        kernel,
        out_shape=jax.ShapeDtypeStruct((ROWS, COLS), bf16),
        in_specs=[smem_spec, smem_spec, any_spec, any_spec, any_spec, any_spec],
        out_specs=pl.BlockSpec(memory_space=pltpu.VMEM),
        scratch_shapes=[
            vmem((ROWS, PAIR), bf16),
            vmem((3 * ROWS, PAIR), bf16),
            vmem((3 * ROWS, PAIR), bf16),
            vmem((2, 2048, COLS), bf16),
            vmem((2, ROWS, 2048), bf16),
            dma((4,)),
            dma((3, 16)), dma((3, 16)),
            dma((2, 2)), dma((2, 2)),
            pltpu.SemaphoreType.REGULAR((4, 2)),
            dma((2,)), dma((2,)),
            dma((2,)), dma((2,)),
            dma((2, 4)), dma((2, 4)),
            dma((2, 4)), dma((2, 4)),
            dma((16,)), dma((16,)),
            dma((CHUNKS, 4)), dma((CHUNKS, 4)),
            dma((CHUNKS, 2, 4)), dma((CHUNKS, 2, 4)),
            dma((CHUNKS, 2, 2)), dma((CHUNKS, 2, 2)),
        ],
        compiler_params=pltpu.CompilerParams(
            collective_id=0, has_side_effects=True, vmem_limit_bytes=56 * 1024 * 1024
        ),
    )(key_tiles, key_counts, queries, keys, values, out_weight)


def solution(mesh):
    in_specs = (
        P(("dp", "head"), None),
        P(("dp", "head"), None),
        P(("dp", "head"), None),
        P("dp", None),
        P("dp"),
        P("dp", "head"),
    )
    out_specs = P("dp", "head")
    return jax.shard_map(local, mesh=mesh, in_specs=in_specs, out_specs=out_specs, check_vma=False)
```

```python
import math

import jax
import jax.numpy as jnp
from jax import lax
from jax.experimental import pallas as pl
from jax.experimental.pallas import tpu as pltpu
from jax.sharding import PartitionSpec as P

HD = 128
TILE = 384
KMAX = 6
GRID_F = 2
ROWS = 768
TOK = 48
PAIR = 256
COLS = 384
DEAD = 1e30
CHUNK = 192
CHUNKS = ROWS // CHUNK
MESH = pl.DeviceIdType.MESH


def kernel(
    tiles_ref, counts_ref, q_hbm, k_hbm, v_hbm, w_hbm, out_ref,
    q_rows, k_ext, v_ext, weight, agat,
    local_sem, a2a_send, a2a_recv, halo_send, halo_recv, known,
    far_send, far_recv, half_send, half_recv, near_send, near_recv, next_send, next_recv, sib_send, sib_recv,
    s1_send, s1_recv, s2_send, s2_recv, s3_send, s3_recv,
):
    dp = lax.axis_index("dp")
    h = lax.axis_index("head")
    z, c = dp // 2, dp % 2
    x, y = h // 4, h % 4
    sibling = dp + 1 - 2 * c

    def remote(src, dst, send, recv, dp_to, h_to):
        return pltpu.make_async_remote_copy(
            src_ref=src, dst_ref=dst, send_sem=send, recv_sem=recv, device_id=(dp_to, h_to), device_id_type=MESH
        )

    has_next, has_prev = dp < 31, dp > 0
    has_up, has_down = z < 15, z > 0
    barrier = pltpu.get_barrier_semaphore()

    def signal(sem, dp_to, h_to):
        pl.semaphore_signal(sem, inc=1, device_id=(dp_to, h_to), device_id_type=MESH)

    def greet(i, carry):
        signal(barrier, dp, (h + i) % 16)
        return carry

    lax.fori_loop(1, 16, greet, 0)
    for there, step in ((has_next, 1), (has_prev, -1), (has_up, 2), (has_down, -2)):
        @pl.when(there)
        def _():
            signal(barrier, (dp + step + 32) % 32, h)

    @pl.when(has_up & has_down)
    def _():
        pl.semaphore_wait(barrier, 19)

    @pl.when(jnp.logical_not(has_up) | jnp.logical_not(has_down))
    def _():
        @pl.when(has_next & has_prev)
        def _():
            pl.semaphore_wait(barrier, 18)

        @pl.when(jnp.logical_not(has_next) | jnp.logical_not(has_prev))
        def _():
            pl.semaphore_wait(barrier, 17)

    def meet_signal(r):
        @pl.when(z + 2**r < 16)
        def _():
            signal(known.at[r, 0], (dp + 2 ** (r + 1)) % 32, h)

        @pl.when(z >= 2**r)
        def _():
            signal(known.at[r, 1], (dp - 2 ** (r + 1) + 32) % 32, h)

    def meet_wait(r):
        @pl.when(z >= 2**r)
        def _():
            pl.semaphore_wait(known.at[r, 0], 1)

        @pl.when(z + 2**r < 16)
        def _():
            pl.semaphore_wait(known.at[r, 1], 1)

    meet_signal(0)

    sources = (k_hbm, v_hbm, q_hbm)
    targets = (k_ext, v_ext, q_rows)
    bases = (ROWS, ROWS, 0)

    def columns_of(head_to):
        return pl.ds(pl.multiple_of(PAIR * head_to, PAIR), PAIR)

    def land(a, head_from):
        return targets[a].at[pl.ds(pl.multiple_of(bases[a] + TOK * head_from, 16), TOK)]

    def a2a_copy(a, i):
        to = (h + i) % 16
        return remote(sources[a].at[:, columns_of(to)], land(a, h), a2a_send.at[a, i], a2a_recv.at[a, i], dp, to)

    def own_copy(a):
        return pltpu.make_async_copy(sources[a].at[:, columns_of(h)], land(a, h), local_sem.at[a])

    def a2a_start(a):
        own_copy(a).start()

        def start_one(i, carry):
            a2a_copy(a, i).start()
            return carry

        lax.fori_loop(1, 16, start_one, 0)

    a2a_start(0)
    a2a_start(1)

    def a2a_wait(a):
        own_copy(a).wait()

        def wait_one(i, carry):
            a2a_copy(a, i).wait_recv()
            return carry

        lax.fori_loop(1, 16, wait_one, 0)

    middle = pl.ds(ROWS, ROWS)
    sides = (pl.ds(0, ROWS), pl.ds(2 * ROWS, ROWS))

    def halo_copy(a, side):
        return remote(
            targets[a].at[middle], targets[a].at[sides[side]], halo_send.at[a, side], halo_recv.at[a, side],
            (dp + 1 + 30 * side) % 32, h,
        )

    def halo_start(a):
        @pl.when(has_next)
        def _():
            halo_copy(a, 0).start()

        @pl.when(has_prev)
        def _():
            halo_copy(a, 1).start()

    def halo_wait_recv(a):
        @pl.when(has_prev)
        def _():
            halo_copy(a, 0).wait_recv()

        @pl.when(has_next)
        def _():
            halo_copy(a, 1).wait_recv()

    def halo_wait_send(a):
        @pl.when(has_next)
        def _():
            halo_copy(a, 0).wait_send()

        @pl.when(has_prev)
        def _():
            halo_copy(a, 1).wait_send()

    @pl.when(jnp.logical_not(has_prev))
    def _():
        k_ext[0:ROWS, :] = jnp.zeros((ROWS, PAIR), jnp.bfloat16)
        v_ext[0:ROWS, :] = jnp.zeros((ROWS, PAIR), jnp.bfloat16)

    @pl.when(jnp.logical_not(has_next))
    def _():
        k_ext[2 * ROWS : 3 * ROWS, :] = jnp.zeros((ROWS, PAIR), jnp.bfloat16)
        v_ext[2 * ROWS : 3 * ROWS, :] = jnp.zeros((ROWS, PAIR), jnp.bfloat16)

    def weight_block(offset, core, first=0, count=128):
        return weight.at[core, pl.ds(pl.multiple_of(128 * ((z + offset + 16) % 16) + first, 64), count)]

    def along(offset, step, sends, recvs, first=0, count=128):
        b = weight_block(offset, c, first, count)
        return remote(b, b, sends, recvs, (dp + 2 * step + 32) % 32, h)

    w_local = pltpu.make_async_copy(w_hbm, weight_block(0, c), local_sem.at[3])
    w_local.start()

    def far_copy(side):
        return along(0, 4 - 8 * side, far_send.at[side], far_recv.at[side])

    def far_arrival(side):
        return along(8 * side - 4, 4 - 8 * side, far_send.at[side], far_recv.at[side])

    def far_start(wraps):
        for side, inside in ((0, z < 12), (1, z >= 4)):
            @pl.when(jnp.logical_not(inside) if wraps else inside)
            def _():
                far_copy(side).start()

    def half_copy(side):
        return along(8 * side - 4, 4 - 8 * side, half_send.at[side], half_recv.at[side], 64 * side, 64)

    def half_arrival(side):
        return along(8, 4 - 8 * side, half_send.at[side], half_recv.at[side], 64 * side, 64)

    def near_copy(m, side):
        return along(4 * m, 1 - 2 * side, near_send.at[side, m], near_recv.at[side, m])

    def near_arrival(m, side):
        return along((4 * m + 15 + 2 * side) % 16, 1 - 2 * side, near_send.at[side, m], near_recv.at[side, m])

    def next_copy(m, side):
        return along((4 * m + 15 + 2 * side) % 16, 1 - 2 * side, next_send.at[side, m], next_recv.at[side, m])

    def next_arrival(m, side):
        return along((4 * m + 14 + 4 * side) % 16, 1 - 2 * side, next_send.at[side, m], next_recv.at[side, m])

    PASSED = ((0, 3), (0, 1))

    def share(offset):
        b = weight_block(offset, c)
        return remote(b, b, sib_send.at[offset], sib_recv.at[offset], sibling, h)

    def far_pass():
        for side in range(2):
            far_arrival(side).wait_recv()
            half_copy(side).start()
        for m in (0, 3, 1):
            for side in range(2):
                near_copy(m, side).start()
        share(12).start()
        share(4).start()

    def half_pass():
        for side in range(2):
            half_arrival(side).wait_recv()
        for side in range(2):
            near_copy(2, side).start()
        share(8).start()

    def near_pass():
        for m in (0, 3, 1, 2):
            for side in range(2):
                near_arrival(m, side).wait_recv()
                if m in PASSED[side]:
                    next_copy(m, side).start()
                share((4 * m + 15 + 2 * side) % 16).start()

    def next_done():
        for side in range(2):
            for m in PASSED[side]:
                next_arrival(m, side).wait_recv()
                share((4 * m + 14 + 4 * side) % 16).start()

    def sibling_done():
        for offset in range(16):
            b = weight_block(offset, 1 - c)
            remote(b, b, sib_send.at[offset], sib_recv.at[offset], sibling, h).wait_recv()

    factor = HD ** -0.5 * math.log2(math.e)

    def bias_of(t):
        count = counts_ref[t]
        out = []
        for b in range(KMAX):
            tile = GRID_F * dp - GRID_F + b
            live = jnp.zeros((), jnp.bool_)
            for j in range(KMAX):
                live = live | ((tiles_ref[t, j] == tile) & (j < count))
            out.append(jnp.where(live, 0.0, -DEAD).astype(jnp.float32))
        return out

    def attend(chunk, hd, bias):
        lanes = slice(hd * HD, hd * HD + HD)
        out_lanes = pl.ds(pl.multiple_of(HD * h, HD), HD)
        lo = chunk * CHUNK
        q = q_rows[lo : lo + CHUNK, lanes]
        scored = [
            lax.dot_general(
                q, k_ext[b * TILE : (b + 1) * TILE, lanes], (((1,), (1,)), ((), ())),
                preferred_element_type=jnp.float32,
            )
            for b in range(KMAX)
        ]
        peak = None
        for b in range(KMAX):
            here = jnp.max(scored[b], axis=1, keepdims=True) + bias[b]
            peak = here if peak is None else jnp.maximum(peak, here)
        total, weighted = None, None
        for b in range(KMAX):
            weights = jnp.exp2((scored[b] - (peak - bias[b])) * factor)
            part_sum = jnp.sum(weights, axis=1, keepdims=True)
            part_out = jnp.dot(
                weights.astype(jnp.bfloat16), v_ext[b * TILE : (b + 1) * TILE, lanes],
                preferred_element_type=jnp.float32,
            )
            total = part_sum if total is None else total + part_sum
            weighted = part_out if weighted is None else weighted + part_out
        agat[hd, lo : lo + CHUNK, out_lanes] = (weighted / total).astype(jnp.bfloat16)

    def place(chunk, i, steps):
        if chunk % 2 == 0:
            return 4 * ((x + steps + 4) % 4) + (y - i + 4) % 4
        return 4 * ((x - i + 4) % 4) + (y + steps + 4) % 4

    def gathered_block(chunk, u):
        return agat.at[:, pl.ds(chunk * CHUNK, CHUNK), pl.ds(pl.multiple_of(HD * u, HD), HD)]

    def hop(chunk, u, to, sends, recvs):
        b = gathered_block(chunk, u)
        return remote(b, b, sends, recvs, dp, to)

    def first_copy(chunk, i):
        return hop(chunk, h, place(chunk, -i, 0), s1_send.at[chunk, i], s1_recv.at[chunk, i])

    def first_arrival(chunk, i):
        return hop(chunk, place(chunk, i, 0), h, s1_send.at[chunk, i], s1_recv.at[chunk, i])

    def second_copy(chunk, i, side):
        return hop(
            chunk, place(chunk, i, 0), place(chunk, 0, 1 - 2 * side),
            s2_send.at[chunk, side, i], s2_recv.at[chunk, side, i],
        )

    def second_arrival(chunk, i, side):
        return hop(
            chunk, place(chunk, i, 2 * side - 1), h, s2_send.at[chunk, side, i], s2_recv.at[chunk, side, i]
        )

    def third_copy(chunk, n, side):
        return hop(
            chunk, place(chunk, n + 2 * side, 2 * side - 1), place(chunk, 0, 1 - 2 * side),
            s3_send.at[chunk, side, n], s3_recv.at[chunk, side, n],
        )

    def third_arrival(chunk, n, side):
        return hop(
            chunk, place(chunk, n + 2 * side, 2), h, s3_send.at[chunk, side, n], s3_recv.at[chunk, side, n]
        )

    def send_first(chunk):
        for i in (2, 1, 3):
            first_copy(chunk, i).start()
        for side in range(2):
            second_copy(chunk, 0, side).start()

    def send_second(chunk):
        for i in (1, 3, 2):
            first_arrival(chunk, i).wait_recv()
            for side in range(2):
                second_copy(chunk, i, side).start()

    def send_third(chunk):
        for i in (0, 1, 3, 2):
            for side in range(2):
                second_arrival(chunk, i, side).wait_recv()
                if i // 2 == side:
                    third_copy(chunk, i % 2, side).start()

    def last_arrivals(chunk):
        for n in range(2):
            for side in range(2):
                third_arrival(chunk, n, side).wait_recv()

    def project(chunk):
        rows = slice(chunk * CHUNK, (chunk + 1) * CHUNK)
        out = None
        for part in range(2):
            term = jnp.dot(agat[part, rows, :], weight[part], preferred_element_type=jnp.float32)
            out = term if out is None else out + term
        out_ref[rows, :] = out.astype(jnp.bfloat16)

    def regrouped_sent():
        for a in range(3):

            def sent_one(i, carry, a=a):
                a2a_copy(a, i).wait_send()
                return carry

            lax.fori_loop(1, 16, sent_one, 0)
        halo_wait_send(0)
        halo_wait_send(1)

    def weight_sent():
        for side in range(2):
            far_copy(side).wait_send()
            half_copy(side).wait_send()
            for m in range(4):
                near_copy(m, side).wait_send()
            for m in PASSED[side]:
                next_copy(m, side).wait_send()
        for offset in range(16):
            share(offset).wait_send()

    def blocks_sent(chunk):
        for i in range(4):
            if i > 0:
                first_copy(chunk, i).wait_send()
            for side in range(2):
                second_copy(chunk, i, side).wait_send()

    def third_sent(chunk):
        for n in range(2):
            for side in range(2):
                third_copy(chunk, n, side).wait_send()

    biases = [bias_of(0), bias_of(1)]

    def attention(chunk):
        for hd in range(2):
            attend(chunk, hd, biases[chunk * CHUNK // TILE])
        send_first(chunk)

    meet_wait(0)
    meet_signal(1)
    a2a_wait(0)
    halo_start(0)
    a2a_start(2)
    meet_wait(1)
    meet_signal(2)
    a2a_wait(1)
    halo_start(1)
    meet_wait(2)
    meet_signal(3)
    w_local.wait()
    share(0).start()
    a2a_wait(2)
    meet_wait(3)
    halo_wait_recv(0)
    halo_wait_recv(1)
    far_start(False)
    far_start(True)
    attention(0)
    attention(1)
    send_second(0)
    attention(2)
    far_pass()
    attention(3)
    send_second(1)
    half_pass()
    send_third(0)
    send_second(2)
    send_third(1)
    send_second(3)
    near_pass()
    send_third(2)
    last_arrivals(0)
    send_third(3)
    regrouped_sent()
    last_arrivals(1)
    next_done()
    sibling_done()
    weight_sent()
    project(0)
    project(1)
    for chunk in range(2):
        blocks_sent(chunk)
    last_arrivals(2)
    project(2)
    for chunk in range(2, CHUNKS):
        blocks_sent(chunk)
    for chunk in range(2):
        third_sent(chunk)
    last_arrivals(3)
    project(3)

    for chunk in range(2, CHUNKS):
        third_sent(chunk)


def local(queries, keys, values, key_tiles, key_counts, out_weight):
    dma = pltpu.SemaphoreType.DMA
    vmem = pltpu.VMEM
    bf16 = jnp.bfloat16
    smem_spec = pl.BlockSpec(memory_space=pltpu.SMEM)
    any_spec = pl.BlockSpec(memory_space=pl.ANY)
    return pl.pallas_call(
        kernel,
        out_shape=jax.ShapeDtypeStruct((ROWS, COLS), bf16),
        in_specs=[smem_spec, smem_spec, any_spec, any_spec, any_spec, any_spec],
        out_specs=pl.BlockSpec(memory_space=pltpu.VMEM),
        scratch_shapes=[
            vmem((ROWS, PAIR), bf16),
            vmem((3 * ROWS, PAIR), bf16),
            vmem((3 * ROWS, PAIR), bf16),
            vmem((2, 2048, COLS), bf16),
            vmem((2, ROWS, 2048), bf16),
            dma((4,)),
            dma((3, 16)), dma((3, 16)),
            dma((2, 2)), dma((2, 2)),
            pltpu.SemaphoreType.REGULAR((4, 2)),
            dma((2,)), dma((2,)),
            dma((2,)), dma((2,)),
            dma((2, 4)), dma((2, 4)),
            dma((2, 4)), dma((2, 4)),
            dma((16,)), dma((16,)),
            dma((CHUNKS, 4)), dma((CHUNKS, 4)),
            dma((CHUNKS, 2, 4)), dma((CHUNKS, 2, 4)),
            dma((CHUNKS, 2, 2)), dma((CHUNKS, 2, 2)),
        ],
        compiler_params=pltpu.CompilerParams(
            collective_id=0, has_side_effects=True, vmem_limit_bytes=56 * 1024 * 1024
        ),
    )(key_tiles, key_counts, queries, keys, values, out_weight)


def solution(mesh):
    in_specs = (
        P(("dp", "head"), None),
        P(("dp", "head"), None),
        P(("dp", "head"), None),
        P("dp", None),
        P("dp"),
        P("dp", "head"),
    )
    out_specs = P("dp", "head")
    return jax.shard_map(local, mesh=mesh, in_specs=in_specs, out_specs=out_specs, check_vma=False)
```

```python
import math

import jax
import jax.numpy as jnp
from jax import lax
from jax.experimental import pallas as pl
from jax.experimental.pallas import tpu as pltpu
from jax.sharding import PartitionSpec as P

HD = 128
TILE = 384
KMAX = 6
GRID_F = 2
ROWS = 768
TOK = 48
PAIR = 256
COLS = 384
DEAD = 1e30
CHUNK = 192
CHUNKS = ROWS // CHUNK
MESH = pl.DeviceIdType.MESH


def kernel(
    tiles_ref, counts_ref, q_hbm, k_hbm, v_hbm, w_hbm, out_ref,
    q_rows, k_ext, v_ext, weight, agat,
    local_sem, a2a_send, a2a_recv, halo_send, halo_recv, known,
    far_send, far_recv, half_send, half_recv, near_send, near_recv, next_send, next_recv, sib_send, sib_recv,
    s1_send, s1_recv, s2_send, s2_recv, s3_send, s3_recv,
):
    dp = lax.axis_index("dp")
    h = lax.axis_index("head")
    z, c = dp // 2, dp % 2
    x, y = h // 4, h % 4
    sibling = dp + 1 - 2 * c

    def remote(src, dst, send, recv, dp_to, h_to):
        return pltpu.make_async_remote_copy(
            src_ref=src, dst_ref=dst, send_sem=send, recv_sem=recv, device_id=(dp_to, h_to), device_id_type=MESH
        )

    has_next, has_prev = dp < 31, dp > 0
    has_up, has_down = z < 15, z > 0
    barrier = pltpu.get_barrier_semaphore()

    def signal(sem, dp_to, h_to):
        pl.semaphore_signal(sem, inc=1, device_id=(dp_to, h_to), device_id_type=MESH)

    def greet(i, carry):
        signal(barrier, dp, (h + i) % 16)
        return carry

    lax.fori_loop(1, 16, greet, 0)
    for there, step in ((has_next, 1), (has_prev, -1), (has_up, 2), (has_down, -2)):
        @pl.when(there)
        def _():
            signal(barrier, (dp + step + 32) % 32, h)

    @pl.when(has_up & has_down)
    def _():
        pl.semaphore_wait(barrier, 19)

    @pl.when(jnp.logical_not(has_up) | jnp.logical_not(has_down))
    def _():
        @pl.when(has_next & has_prev)
        def _():
            pl.semaphore_wait(barrier, 18)

        @pl.when(jnp.logical_not(has_next) | jnp.logical_not(has_prev))
        def _():
            pl.semaphore_wait(barrier, 17)

    def meet_signal(r):
        @pl.when(z + 2**r < 16)
        def _():
            signal(known.at[r, 0], (dp + 2 ** (r + 1)) % 32, h)

        @pl.when(z >= 2**r)
        def _():
            signal(known.at[r, 1], (dp - 2 ** (r + 1) + 32) % 32, h)

    def meet_wait(r):
        @pl.when(z >= 2**r)
        def _():
            pl.semaphore_wait(known.at[r, 0], 1)

        @pl.when(z + 2**r < 16)
        def _():
            pl.semaphore_wait(known.at[r, 1], 1)

    meet_signal(0)

    sources = (k_hbm, v_hbm, q_hbm)
    targets = (k_ext, v_ext, q_rows)
    bases = (ROWS, ROWS, 0)

    def columns_of(head_to):
        return pl.ds(pl.multiple_of(PAIR * head_to, PAIR), PAIR)

    def land(a, head_from):
        return targets[a].at[pl.ds(pl.multiple_of(bases[a] + TOK * head_from, 16), TOK)]

    def a2a_copy(a, i):
        to = (h + i) % 16
        return remote(sources[a].at[:, columns_of(to)], land(a, h), a2a_send.at[a, i], a2a_recv.at[a, i], dp, to)

    def own_copy(a):
        return pltpu.make_async_copy(sources[a].at[:, columns_of(h)], land(a, h), local_sem.at[a])

    def a2a_start(a):
        own_copy(a).start()

        def start_one(i, carry):
            a2a_copy(a, i).start()
            return carry

        lax.fori_loop(1, 16, start_one, 0)

    a2a_start(0)
    a2a_start(1)

    def a2a_wait(a):
        own_copy(a).wait()

        def wait_one(i, carry):
            a2a_copy(a, i).wait_recv()
            return carry

        lax.fori_loop(1, 16, wait_one, 0)

    middle = pl.ds(ROWS, ROWS)
    sides = (pl.ds(0, ROWS), pl.ds(2 * ROWS, ROWS))

    def halo_copy(a, side):
        return remote(
            targets[a].at[middle], targets[a].at[sides[side]], halo_send.at[a, side], halo_recv.at[a, side],
            (dp + 1 + 30 * side) % 32, h,
        )

    def halo_start(a):
        @pl.when(has_next)
        def _():
            halo_copy(a, 0).start()

        @pl.when(has_prev)
        def _():
            halo_copy(a, 1).start()

    def halo_wait_recv(a):
        @pl.when(has_prev)
        def _():
            halo_copy(a, 0).wait_recv()

        @pl.when(has_next)
        def _():
            halo_copy(a, 1).wait_recv()

    def halo_wait_send(a):
        @pl.when(has_next)
        def _():
            halo_copy(a, 0).wait_send()

        @pl.when(has_prev)
        def _():
            halo_copy(a, 1).wait_send()

    @pl.when(jnp.logical_not(has_prev))
    def _():
        k_ext[0:ROWS, :] = jnp.zeros((ROWS, PAIR), jnp.bfloat16)
        v_ext[0:ROWS, :] = jnp.zeros((ROWS, PAIR), jnp.bfloat16)

    @pl.when(jnp.logical_not(has_next))
    def _():
        k_ext[2 * ROWS : 3 * ROWS, :] = jnp.zeros((ROWS, PAIR), jnp.bfloat16)
        v_ext[2 * ROWS : 3 * ROWS, :] = jnp.zeros((ROWS, PAIR), jnp.bfloat16)

    def weight_block(offset, core, first=0, count=128):
        return weight.at[core, pl.ds(pl.multiple_of(128 * ((z + offset + 16) % 16) + first, 64), count)]

    def along(offset, step, sends, recvs, first=0, count=128):
        b = weight_block(offset, c, first, count)
        return remote(b, b, sends, recvs, (dp + 2 * step + 32) % 32, h)

    w_local = pltpu.make_async_copy(w_hbm, weight_block(0, c), local_sem.at[3])
    w_local.start()

    def far_copy(side):
        return along(0, 4 - 8 * side, far_send.at[side], far_recv.at[side])

    def far_arrival(side):
        return along(8 * side - 4, 4 - 8 * side, far_send.at[side], far_recv.at[side])

    def far_start(wraps):
        for side, inside in ((0, z < 12), (1, z >= 4)):
            @pl.when(jnp.logical_not(inside) if wraps else inside)
            def _():
                far_copy(side).start()

    def half_copy(side):
        return along(8 * side - 4, 4 - 8 * side, half_send.at[side], half_recv.at[side], 64 * side, 64)

    def half_arrival(side):
        return along(8, 4 - 8 * side, half_send.at[side], half_recv.at[side], 64 * side, 64)

    def near_copy(m, side):
        return along(4 * m, 1 - 2 * side, near_send.at[side, m], near_recv.at[side, m])

    def near_arrival(m, side):
        return along((4 * m + 15 + 2 * side) % 16, 1 - 2 * side, near_send.at[side, m], near_recv.at[side, m])

    def next_copy(m, side):
        return along((4 * m + 15 + 2 * side) % 16, 1 - 2 * side, next_send.at[side, m], next_recv.at[side, m])

    def next_arrival(m, side):
        return along((4 * m + 14 + 4 * side) % 16, 1 - 2 * side, next_send.at[side, m], next_recv.at[side, m])

    PASSED = ((0, 3), (0, 1))

    def share(offset):
        b = weight_block(offset, c)
        return remote(b, b, sib_send.at[offset], sib_recv.at[offset], sibling, h)

    def far_pass():
        for side in range(2):
            far_arrival(side).wait_recv()
            half_copy(side).start()
        for m in (0, 3, 1):
            for side in range(2):
                near_copy(m, side).start()
        share(12).start()
        share(4).start()

    def half_pass():
        for side in range(2):
            half_arrival(side).wait_recv()
        for side in range(2):
            near_copy(2, side).start()
        share(8).start()

    def near_pass():
        for m in (0, 3, 1, 2):
            for side in range(2):
                near_arrival(m, side).wait_recv()
                if m in PASSED[side]:
                    next_copy(m, side).start()
                share((4 * m + 15 + 2 * side) % 16).start()

    def next_done():
        for side in range(2):
            for m in PASSED[side]:
                next_arrival(m, side).wait_recv()
                share((4 * m + 14 + 4 * side) % 16).start()

    def sibling_done():
        for offset in range(16):
            b = weight_block(offset, 1 - c)
            remote(b, b, sib_send.at[offset], sib_recv.at[offset], sibling, h).wait_recv()

    factor = HD ** -0.5 * math.log2(math.e)

    def bias_of(t):
        count = counts_ref[t]
        out = []
        for b in range(KMAX):
            tile = GRID_F * dp - GRID_F + b
            live = jnp.zeros((), jnp.bool_)
            for j in range(KMAX):
                live = live | ((tiles_ref[t, j] == tile) & (j < count))
            out.append(jnp.where(live, 0.0, -DEAD).astype(jnp.float32))
        return out

    def attend(chunk, hd, bias):
        lanes = slice(hd * HD, hd * HD + HD)
        out_lanes = pl.ds(pl.multiple_of(HD * h, HD), HD)
        lo = chunk * CHUNK
        q = q_rows[lo : lo + CHUNK, lanes]
        scored = [
            lax.dot_general(
                q, k_ext[b * TILE : (b + 1) * TILE, lanes], (((1,), (1,)), ((), ())),
                preferred_element_type=jnp.float32,
            )
            for b in range(KMAX)
        ]
        peak = None
        for b in range(KMAX):
            here = jnp.max(scored[b], axis=1, keepdims=True) + bias[b]
            peak = here if peak is None else jnp.maximum(peak, here)
        total, weighted = None, None
        for b in range(KMAX):
            weights = jnp.exp2((scored[b] - (peak - bias[b])) * factor)
            part_sum = jnp.sum(weights, axis=1, keepdims=True)
            part_out = jnp.dot(
                weights.astype(jnp.bfloat16), v_ext[b * TILE : (b + 1) * TILE, lanes],
                preferred_element_type=jnp.float32,
            )
            total = part_sum if total is None else total + part_sum
            weighted = part_out if weighted is None else weighted + part_out
        agat[hd, lo : lo + CHUNK, out_lanes] = (weighted / total).astype(jnp.bfloat16)

    def place(chunk, i, steps):
        if chunk % 2 == 0:
            return 4 * ((x + steps + 4) % 4) + (y - i + 4) % 4
        return 4 * ((x - i + 4) % 4) + (y + steps + 4) % 4

    def gathered_block(chunk, u):
        return agat.at[:, pl.ds(chunk * CHUNK, CHUNK), pl.ds(pl.multiple_of(HD * u, HD), HD)]

    def hop(chunk, u, to, sends, recvs):
        b = gathered_block(chunk, u)
        return remote(b, b, sends, recvs, dp, to)

    def first_copy(chunk, i):
        return hop(chunk, h, place(chunk, -i, 0), s1_send.at[chunk, i], s1_recv.at[chunk, i])

    def first_arrival(chunk, i):
        return hop(chunk, place(chunk, i, 0), h, s1_send.at[chunk, i], s1_recv.at[chunk, i])

    def second_copy(chunk, i, side):
        return hop(
            chunk, place(chunk, i, 0), place(chunk, 0, 1 - 2 * side),
            s2_send.at[chunk, side, i], s2_recv.at[chunk, side, i],
        )

    def second_arrival(chunk, i, side):
        return hop(
            chunk, place(chunk, i, 2 * side - 1), h, s2_send.at[chunk, side, i], s2_recv.at[chunk, side, i]
        )

    def third_copy(chunk, n, side):
        return hop(
            chunk, place(chunk, n + 2 * side, 2 * side - 1), place(chunk, 0, 1 - 2 * side),
            s3_send.at[chunk, side, n], s3_recv.at[chunk, side, n],
        )

    def third_arrival(chunk, n, side):
        return hop(
            chunk, place(chunk, n + 2 * side, 2), h, s3_send.at[chunk, side, n], s3_recv.at[chunk, side, n]
        )

    def send_first(chunk):
        for i in (2, 1, 3):
            first_copy(chunk, i).start()
        for side in range(2):
            second_copy(chunk, 0, side).start()

    def send_second(chunk):
        for i in (1, 3, 2):
            first_arrival(chunk, i).wait_recv()
            for side in range(2):
                second_copy(chunk, i, side).start()

    def send_third(chunk):
        for i in (0, 1, 3, 2):
            for side in range(2):
                second_arrival(chunk, i, side).wait_recv()
                if i // 2 == side:
                    third_copy(chunk, i % 2, side).start()

    def last_arrivals(chunk):
        for n in range(2):
            for side in range(2):
                third_arrival(chunk, n, side).wait_recv()

    def project(chunk):
        rows = slice(chunk * CHUNK, (chunk + 1) * CHUNK)
        out = None
        for part in range(2):
            term = jnp.dot(agat[part, rows, :], weight[part], preferred_element_type=jnp.float32)
            out = term if out is None else out + term
        out_ref[rows, :] = out.astype(jnp.bfloat16)

    def regrouped_sent():
        for a in range(3):

            def sent_one(i, carry, a=a):
                a2a_copy(a, i).wait_send()
                return carry

            lax.fori_loop(1, 16, sent_one, 0)
        halo_wait_send(0)
        halo_wait_send(1)

    def weight_sent():
        for side in range(2):
            far_copy(side).wait_send()
            half_copy(side).wait_send()
            for m in range(4):
                near_copy(m, side).wait_send()
            for m in PASSED[side]:
                next_copy(m, side).wait_send()
        for offset in range(16):
            share(offset).wait_send()

    def blocks_sent(chunk):
        for i in range(4):
            if i > 0:
                first_copy(chunk, i).wait_send()
            for side in range(2):
                second_copy(chunk, i, side).wait_send()

    def third_sent(chunk):
        for n in range(2):
            for side in range(2):
                third_copy(chunk, n, side).wait_send()

    biases = [bias_of(0), bias_of(1)]

    def attention(chunk):
        for hd in range(2):
            attend(chunk, hd, biases[chunk * CHUNK // TILE])
        send_first(chunk)

    meet_wait(0)
    meet_signal(1)
    a2a_wait(0)
    halo_start(0)
    a2a_start(2)
    meet_wait(1)
    meet_signal(2)
    a2a_wait(1)
    halo_start(1)
    meet_wait(2)
    meet_signal(3)
    a2a_wait(2)
    w_local.wait()
    share(0).start()
    far_start(False)
    meet_wait(3)
    far_start(True)
    halo_wait_recv(0)
    halo_wait_recv(1)
    attention(0)
    attention(1)
    send_second(0)
    attention(2)
    far_pass()
    attention(3)
    send_second(1)
    half_pass()
    send_third(0)
    send_second(2)
    send_third(1)
    send_second(3)
    near_pass()
    send_third(2)
    last_arrivals(0)
    send_third(3)
    regrouped_sent()
    last_arrivals(1)
    next_done()
    sibling_done()
    weight_sent()
    project(0)
    project(1)
    for chunk in range(2):
        blocks_sent(chunk)
    last_arrivals(2)
    project(2)
    for chunk in range(2, CHUNKS):
        blocks_sent(chunk)
    for chunk in range(2):
        third_sent(chunk)
    last_arrivals(3)
    project(3)

    for chunk in range(2, CHUNKS):
        third_sent(chunk)


def local(queries, keys, values, key_tiles, key_counts, out_weight):
    dma = pltpu.SemaphoreType.DMA
    vmem = pltpu.VMEM
    bf16 = jnp.bfloat16
    smem_spec = pl.BlockSpec(memory_space=pltpu.SMEM)
    any_spec = pl.BlockSpec(memory_space=pl.ANY)
    return pl.pallas_call(
        kernel,
        out_shape=jax.ShapeDtypeStruct((ROWS, COLS), bf16),
        in_specs=[smem_spec, smem_spec, any_spec, any_spec, any_spec, any_spec],
        out_specs=pl.BlockSpec(memory_space=pltpu.VMEM),
        scratch_shapes=[
            vmem((ROWS, PAIR), bf16),
            vmem((3 * ROWS, PAIR), bf16),
            vmem((3 * ROWS, PAIR), bf16),
            vmem((2, 2048, COLS), bf16),
            vmem((2, ROWS, 2048), bf16),
            dma((4,)),
            dma((3, 16)), dma((3, 16)),
            dma((2, 2)), dma((2, 2)),
            pltpu.SemaphoreType.REGULAR((4, 2)),
            dma((2,)), dma((2,)),
            dma((2,)), dma((2,)),
            dma((2, 4)), dma((2, 4)),
            dma((2, 4)), dma((2, 4)),
            dma((16,)), dma((16,)),
            dma((CHUNKS, 4)), dma((CHUNKS, 4)),
            dma((CHUNKS, 2, 4)), dma((CHUNKS, 2, 4)),
            dma((CHUNKS, 2, 2)), dma((CHUNKS, 2, 2)),
        ],
        compiler_params=pltpu.CompilerParams(
            collective_id=0, has_side_effects=True, vmem_limit_bytes=56 * 1024 * 1024
        ),
    )(key_tiles, key_counts, queries, keys, values, out_weight)


def solution(mesh):
    in_specs = (
        P(("dp", "head"), None),
        P(("dp", "head"), None),
        P(("dp", "head"), None),
        P("dp", None),
        P("dp"),
        P("dp", "head"),
    )
    out_specs = P("dp", "head")
    return jax.shard_map(local, mesh=mesh, in_specs=in_specs, out_specs=out_specs, check_vma=False)
```
